512 devices in a mesh: prow: 32 (over z, x), pcol: 16 (over y, core).
Axes of the slice: x: 4, y: 8, z: 8, core: 2. Of those that a mesh axis runs over, the one named last changes fastest.
Arguments:
- matrix: float32 [24576, 12288], P('prow', 'pcol'), may hold values from -6 to 6
- pivots: int32 [2, 256], replicated, may hold values from 0 to 24575, as said below
- lower_inv: float32 [2, 256, 256], replicated, as said below
- upper_inv: float32 [2, 256, 256], replicated, as said below
Outputs:
- factored: float32 [24576, 12288], P('prow', 'pcol')
The draws below stay inside these ranges and needn't reach their ends.
Inputs may be any that keep to these rules, and one draw needn't show every extreme that they name: `pivots`: for each panel p the 256 entries are distinct; entry j is either the row p * 768 + j itself or a row that lies outside the diagonal rows of panels 0..p. `lower_inv`: each block is unit lower triangular. `upper_inv`: each block is upper triangular with positive diagonal.
All inputs are finite; a program needn't handle non-finite values.
Results may differ from the reference program's by a relative error of at most 0.0001.
Values sent between devices are 32-bit elements; how exact they have to be, the bound alone decides.
No kernel may reach another device: no remote copies, remote signals or barrier semaphores. Data moves between devices by JAX's collectives and lax.ppermute only.
A program may use at most 64 MiB of HBM per device.

```python
import math
import jax
import jax.numpy as jnp
from jax import lax

NB = 256
ROWS_DEV = 768
COLS_DEV = 768
ROWS = 24576
COLS = 12288


def draw_pivots(key, part):
    key = jax.random.fold_in(key, 1)
    row_pos = jnp.arange(ROWS, dtype=jnp.int32)
    column_ids = jnp.arange(NB, dtype=jnp.int32)
    lists = []
    for panel_no in range(2):
        sub_key = jax.random.fold_in(key, panel_no)
        ranks = jax.random.permutation(jax.random.fold_in(sub_key, 7), ROWS).astype(jnp.int32)
        banned = jnp.zeros((ROWS,), bool)
        for earlier in range(panel_no + 1):
            start = earlier * ROWS_DEV
            banned = banned | (row_pos >= start) & (row_pos < start + NB)
        scores = jnp.where(banned, ranks + ROWS, ranks)
        if panel_no == 1:
            scores = jnp.where(row_pos == ROWS - 1, -1, scores)
        chosen = jnp.argsort(scores, stable=True)[:NB].astype(jnp.int32)
        stay_here = jax.random.randint(jax.random.fold_in(sub_key, 9), (NB,), 0, 4) == 0
        if panel_no == 0:
            stay_here = stay_here | (column_ids == 0)
        else:
            stay_here = stay_here & (column_ids != 0)
        lists.append(jnp.where(stay_here, panel_no * ROWS_DEV + column_ids, chosen))
    return jnp.stack(lists).astype(jnp.int32)


def draw_lower_inv(key, part):
    key = jax.random.fold_in(key, 2)
    noise = jax.random.normal(key, (2, NB, NB), jnp.float32)
    row_ids = jnp.arange(NB)[:, None]
    col_ids = jnp.arange(NB)[None, :]
    below = (row_ids > col_ids)[None]
    unit = (row_ids == col_ids)[None].astype(jnp.float32)
    return unit + jnp.where(below, noise * (0.5 / math.sqrt(NB)), 0.0)


def draw_upper_inv(key, part):
    key = jax.random.fold_in(key, 3)
    noise = jax.random.normal(jax.random.fold_in(key, 1), (2, NB, NB), jnp.float32)
    scales = jnp.exp(jax.random.uniform(jax.random.fold_in(key, 2), (2, NB, NB), jnp.float32, math.log(0.5), math.log(2.0)))
    row_ids = jnp.arange(NB)[:, None]
    col_ids = jnp.arange(NB)[None, :]
    above = (row_ids < col_ids)[None]
    on_diag = (row_ids == col_ids)[None]
    blocks = jnp.where(on_diag, scales, jnp.where(above, noise * (0.5 / math.sqrt(NB)), 0.0))
    return blocks * (0.5 / math.sqrt(NB))


def block_levels(rng, extent, shards, least, largest):
    level = 1.0
    for dim, blocks in shards:
        draws = jax.random.uniform(jax.random.fold_in(jax.random.fold_in(rng, 6), dim), (blocks,), jnp.float32, least / len(shards), largest / len(shards))
        level = level * jnp.repeat(jnp.exp(draws), extent[dim] // blocks).reshape((-1,) + (1,) * (len(extent) - 1 - dim))
    return level


def normal_values(key, dims, scale, reach, cuts=(), held_as=jnp.bfloat16):
    loudness = block_levels(key, dims, cuts, -0.22, 0.18) if cuts else 1.0
    result = jax.random.normal(key, dims, jnp.float32) * scale * loudness
    return jnp.minimum(jnp.maximum(result, -reach), reach).astype(held_as)


def setup_inputs(seed: int = 0) -> dict:
    streams_of = jax.random.split(jax.random.key(seed), 5)
    return {
        "matrix": normal_values(streams_of[0], (ROWS, COLS), 1.0, 6.0, ((0, 32), (1, 16)), jnp.float32),
        "pivots": draw_pivots(jax.random.fold_in(streams_of[4], 71), 0),
        "lower_inv": draw_lower_inv(jax.random.fold_in(streams_of[4], 71), 0),
        "upper_inv": draw_upper_inv(jax.random.fold_in(streams_of[4], 71), 0),
    }


def reference(matrix, pivots, lower_inv, upper_inv):
    current = matrix
    rows_total = current.shape[0]
    cols_total = current.shape[1]
    row_pos = jnp.arange(rows_total)
    col_pos = jnp.arange(cols_total)
    row_done = jnp.zeros((rows_total,), bool)
    col_done = jnp.zeros((cols_total,), bool)
    for panel_no in range(2):
        row_start = panel_no * ROWS_DEV
        col_start = panel_no * COLS_DEV
        row_done = row_done | ((row_pos >= row_start) & (row_pos < row_start + NB))
        col_done = col_done | ((col_pos >= col_start) & (col_pos < col_start + NB))
        pivot_list = pivots[panel_no]
        new_rows = current[pivot_list]
        old_rows = current[row_start:row_start + NB]
        current = current.at[pivot_list].set(old_rows)
        current = current.at[row_start:row_start + NB].set(new_rows)
        upper_rows = jnp.dot(lower_inv[panel_no], new_rows, precision=lax.Precision.HIGHEST, preferred_element_type=jnp.float32)
        row_block = jnp.where(col_done[None, :], new_rows, upper_rows)
        lower_cols = jnp.dot(current[:, col_start:col_start + NB], upper_inv[panel_no], precision=lax.Precision.HIGHEST, preferred_element_type=jnp.float32)
        rank_update = jnp.dot(lower_cols, row_block, precision=lax.Precision.HIGHEST, preferred_element_type=jnp.float32)
        keep_mask = (~row_done)[:, None] & (~col_done)[None, :]
        current = jnp.where(keep_mask, current - rank_update, current)
        panel_new = jnp.where(row_done[:, None], current[:, col_start:col_start + NB], lower_cols)
        current = current.at[:, col_start:col_start + NB].set(panel_new)
        current = current.at[row_start:row_start + NB].set(row_block)
    return current
```

```python
import functools

import jax
import jax.numpy as jnp
from jax import lax
from jax.experimental import pallas as pl
from jax.experimental.pallas import tpu as pltpu
from jax.sharding import Mesh, PartitionSpec as P

HIGHEST = lax.Precision.HIGHEST
F32 = jnp.float32
NB = 256
RD = 768
PROW = ("z", "x")
PCOL = ("y", "core")
NP = 32


def hdot(a, b):
    return jnp.dot(a, b, precision=HIGHEST, preferred_element_type=F32)


def iota(shape, dim):
    return lax.broadcasted_iota(jnp.int32, shape, dim)


def f(mask):
    return jnp.where(mask, F32(1.0), F32(0.0))


def sum_rows(x):
    return jnp.sum(x, axis=0, keepdims=True)


def sum_cols(x):
    return jnp.sum(x, axis=1, keepdims=True)


def owner_of(row):
    return ((row >> 8) * 171) >> 9


def index_math(pr, pc):
    p0r, p1r = pr[0:1, :], pr[1:2, :]
    p0c, p1c = pc[:, 0:1], pc[:, 1:2]
    sub, lane = iota((NB, NB), 0), iota((NB, NB), 1)
    lr, lc = iota((1, NB), 1), iota((NB, 1), 0)
    m_kj = f(p0c == lane + RD)
    n_kj = f(p0c == p1r)
    m_jk = f(p0r == sub + RD)
    n_jk = f(p0r == p1c)
    p1rf, p1cf = p1r.astype(F32), p1c.astype(F32)

    def dest(p0, p1, ids, has_m, has_n, piv_m, has_mk):
        stay0 = (p0 == ids) | (has_n > 0)
        end0 = jnp.where(has_m > 0, piv_m.astype(jnp.int32), p0)
        stay1 = (p1 == ids + RD) | (has_mk > 0)
        out = []
        for stay, end in ((stay0, end0), (stay1, p1)):
            own = owner_of(end)
            out.append((jnp.where(stay, NP, own), end - own * RD))
        return out

    has_m_c, has_n_c = sum_cols(m_kj), sum_cols(n_kj)
    has_m_r, has_n_r = sum_rows(m_jk), sum_rows(n_jk)
    has_mk_r, has_nk_r = sum_rows(m_kj), sum_rows(n_kj)
    has_mk_c, has_nk_c = sum_cols(m_jk), sum_cols(n_jk)
    dest_r = dest(p0r, p1r, lr, has_m_r, has_n_r, sum_rows(m_jk * p1cf), has_mk_r)
    dest_c = dest(p0c, p1c, lc, has_m_c, has_n_c, sum_cols(m_kj * p1rf), has_mk_c)
    ranks_r, ranks_c, pos_r, pos_c = [], [], [], []
    for g in range(2):
        key_r = dest_r[g][0] * NB + lr
        key_c = dest_c[g][0] * NB + lc
        rank_r = sum_rows(f(key_c < key_r)).astype(jnp.int32)
        rank_c = sum_cols(f(key_r < key_c)).astype(jnp.int32)
        ranks_r.append(rank_r)
        ranks_c.append(rank_c)
        pos_r.append(((rank_r & 31) * 16 + g * 8 + (rank_r >> 5)).astype(F32))
        pos_c.append(((rank_c & 31) * 16 + g * 8 + (rank_c >> 5)).astype(F32))
    w_r = jnp.where(has_mk_r > 0, sum_rows(m_kj * pos_c[0]), pos_r[1])
    w_c = jnp.where(has_mk_c > 0, sum_cols(m_jk * pos_r[0]), pos_c[1])
    src0 = jnp.where(
        has_m_c > 0,
        sum_cols(m_kj * pos_r[1]),
        jnp.where(has_n_c > 0, sum_cols(n_kj * w_r), pos_c[0]),
    )
    src1 = jnp.where(has_nk_c > 0, sum_cols(n_jk * pos_r[0]), w_c)
    rows, cols = [], []
    for g in range(2):
        rows += [ranks_r[g], dest_r[g][0], dest_r[g][1]]
        cols += [ranks_c[g], dest_c[g][0], dest_c[g][1]]
    cols += [src0.astype(jnp.int32), src1.astype(jnp.int32)]
    return rows, cols


def pack_kernel(ids, pr_ref, pc_ref, a_ref, ext_ref, old_ref, ir_ref, ic_ref):
    me = ids[0]
    rows, cols = index_math(pr_ref[...], pc_ref[...])
    for n, v in enumerate(rows):
        ir_ref[n : n + 1, :] = v
    ir_ref[6:8, :] = jnp.zeros((2, NB), jnp.int32)
    for n, v in enumerate(cols):
        ic_ref[:, n : n + 1] = v
    line = iota((2 * NP, NB), 0)
    pick = jnp.zeros((2 * NP, RD), F32)
    for g in range(2):
        rank, own = rows[3 * g], rows[3 * g + 1]
        s = f(((line & 1) == g) & ((rank & 31) == (line >> 1)) & (own == me))
        t = f(cols[3 * g + 2] == iota((NB, RD), 1))
        pick = pick + jnp.dot(
            s.astype(jnp.bfloat16), t.astype(jnp.bfloat16), preferred_element_type=F32
        )
    ext_ref[...] = hdot(pick, a_ref[...])
    line = iota((NB, NB), 0)
    rank = jnp.where(me == 1, rows[3], rows[0])
    perm = f(rank == (line >> 3) + NP * (line & 7))
    old_ref[...] = hdot(perm, a_ref[0:NB, :])


def turn_kernel(ids, ir_ref, ic_ref, ext_ref, old0_ref, old1_ref, x_ref, ret_ref):
    me = ids[0]
    line = iota((16, NB), 0)
    want = me + NP * (line & 7)
    own = jnp.zeros((16, 1), F32)
    for g in range(2):
        hit = f((ir_ref[3 * g : 3 * g + 1, :] == want) & ((line >> 3) == g))
        own = own + sum_cols(hit * ir_ref[3 * g + 1 : 3 * g + 2, :].astype(F32))
    own = own.astype(jnp.int32)
    old = jnp.concatenate([old0_ref[...], old1_ref[...]], axis=0)
    lane = iota((16, 2 * NP), 1)
    pick = f((own == (lane >> 1)) & ((iota((16, 2 * NP), 0) >> 3) == (lane & 1)))
    x_ref[...] = jnp.where(own == NP, old, hdot(pick, ext_ref[...]))
    want = me + NP * (iota((NB, 16), 1) & 7)
    own = jnp.zeros((1, 16), F32)
    for g in range(2):
        hit = f((ic_ref[:, 3 * g : 3 * g + 1] == want) & ((iota((NB, 16), 1) >> 3) == g))
        own = own + sum_rows(hit * ic_ref[:, 3 * g + 1 : 3 * g + 2].astype(F32))
    own = own.astype(jnp.int32)
    line = iota((2 * NP, 16), 0)
    give = f((own == (line >> 1)) & ((iota((2 * NP, 16), 1) >> 3) == (line & 1)))
    ret_ref[...] = hdot(give, old)


def final_kernel(
    ids, ir_ref, ic_ref, a_ref, c0_ref, c1_ref, x_ref, xc0_ref, xc1_ref,
    ret_ref, rc0_ref, rc1_ref, li_ref, ui_ref, out_ref,
):
    me, col = ids[0], ids[1]
    put = jnp.zeros((RD, 2 * NP), F32)
    for g in range(2):
        own, loc = ir_ref[3 * g + 1 : 3 * g + 2, :], ir_ref[3 * g + 2 : 3 * g + 3, :]
        t = f((own == me) & (loc == iota((RD, NB), 0)))
        lane = iota((NB, 2 * NP), 1)
        s = f(((ic_ref[:, 3 * g : 3 * g + 1] & 31) == (lane >> 1)) & ((lane & 1) == g))
        put = put + jnp.dot(
            t.astype(jnp.bfloat16), s.astype(jnp.bfloat16), preferred_element_type=F32
        )
    moved = sum_cols(put) > 0
    perm0 = f(ic_ref[:, 6:7] == iota((NB, 2 * NB), 1))
    perm1 = f(ic_ref[:, 7:8] == iota((NB, 2 * NB), 1))
    new0 = hdot(perm0, x_ref[...])
    new1 = hdot(perm1, x_ref[...])
    c0 = jnp.where(moved, hdot(put, rc0_ref[...]), c0_ref[...])
    c1 = jnp.where(moved, hdot(put, rc1_ref[...]), c1_ref[...])
    low0 = hdot(c0, ui_ref[0])
    u0 = hdot(li_ref[0], new0)
    u0c1 = hdot(li_ref[0], hdot(perm0, xc1_ref[...]))
    low1 = hdot(c1 - hdot(low0, u0c1), ui_ref[1])
    diag = hdot(hdot(perm1, xc0_ref[...]), ui_ref[0])
    next1 = new1 - hdot(diag, u0)
    u1 = hdot(li_ref[1], next1)
    base = jnp.where(moved, hdot(put, ret_ref[...]), a_ref[...])
    out_ref[...] = base - hdot(low0, u0) - hdot(low1, u1)

    @pl.when(col == 0)
    def _():
        out_ref[:, 0:NB] = low0

    @pl.when(col == 1)
    def _():
        out_ref[:, 0:NB] = low1

    @pl.when(me == 0)
    def _():
        out_ref[0:NB, :] = u0

        @pl.when(col == 0)
        def _():
            out_ref[0:NB, 0:NB] = new0[:, 0:NB]

    @pl.when(me == 1)
    def _():
        out_ref[0:NB, :] = u1

        @pl.when(col == 0)
        def _():
            out_ref[0:NB, 0:NB] = diag

        @pl.when(col == 1)
        def _():
            out_ref[0:NB, 0:NB] = next1[:, 0:NB]


def call(kernel, outs, ids, *args):
    vmem = pl.BlockSpec(memory_space=pltpu.VMEM)
    return pl.pallas_call(
        kernel,
        out_shape=outs,
        in_specs=[pl.BlockSpec(memory_space=pltpu.SMEM)] + [vmem] * len(args),
        out_specs=jax.tree.map(lambda _: vmem, outs),
        compiler_params=pltpu.CompilerParams(vmem_limit_bytes=48 * 1024 * 1024),
    )(ids, *args)


def spread(v, axis, n):
    return lax.all_to_all(jnp.broadcast_to(v[None], (n,) + v.shape), axis, 0, 0)


def from_first(v, axis, n):
    mine = jnp.where(lax.axis_index(axis) == 0, v, jnp.zeros_like(v))
    for k in (4, 3, 5, 2, 6, 1, 7):
        mine = mine + lax.ppermute(v, axis, [(0, k)])
    return mine


def shape(*dims, dtype=F32):
    return jax.ShapeDtypeStruct(dims, dtype)


def fast(matrix, pivots, lower_inv, upper_inv):
    prow_idx = lax.axis_index(PROW).astype(jnp.int32)
    pcol_idx = lax.axis_index(PCOL).astype(jnp.int32)
    ids = jnp.stack([prow_idx, pcol_idx])
    panel = matrix[:, :NB]
    part = RD // 8
    piece = jnp.where(lax.axis_index("y") == 0, panel[:part], jnp.zeros((part, NB), F32))
    for k in (4, 3, 5, 2, 6, 1, 7):
        piece = piece + lax.ppermute(panel[part * k : part * (k + 1)], "y", [(0, k)])
    raw = spread(piece, "y", 8).reshape(RD, NB)
    ext, old, ir, ic = call(
        pack_kernel,
        (shape(2 * NP, RD), shape(NB, RD), shape(8, NB, dtype=jnp.int32), shape(NB, 8, dtype=jnp.int32)),
        ids, pivots, pivots.T, matrix,
    )
    ext_in = lax.all_to_all(ext.reshape(NP, 2, RD), PROW, 0, 0).reshape(2 * NP, RD)
    old_in = lax.all_to_all(old.reshape(NP, 8, RD), PROW, 0, 0)
    x16, ret = call(
        turn_kernel, (shape(16, RD), shape(2 * NP, RD)), ids, ir, ic, ext_in, old_in[0], old_in[1]
    )
    side = from_first(jnp.concatenate([x16[:, :NB], ret[:, :NB]], axis=0), "y", 8)
    x_wide = jnp.concatenate([x16, side[:16]], axis=1)
    ret_wide = jnp.concatenate([ret, side[16:]], axis=1)
    ret_in = lax.all_to_all(ret_wide.reshape(NP, 2, RD + NB), PROW, 0, 0).reshape(2 * NP, RD + NB)
    x_z = spread(x_wide, "z", 8)
    x_all = spread(x_z, "x", 4)
    x_all = x_all.transpose(1, 0, 2, 3).reshape(2 * NB, RD + NB)
    here = jnp.concatenate([x_all[:, RD:], ret_in[:, RD:]], axis=0)
    both = [(0, 1), (1, 0)]
    there = lax.ppermute(here, "core", both)
    raw_there = lax.ppermute(raw, "core", both)
    first = lax.axis_index("core") == 0
    c0, c1 = jnp.where(first, raw, raw_there), jnp.where(first, raw_there, raw)
    s0, s1 = jnp.where(first, here, there), jnp.where(first, there, here)
    return call(
        final_kernel, shape(RD, RD), ids, ir, ic, matrix, c0, c1, x_all[:, :RD],
        s0[: 2 * NB], s1[: 2 * NB], ret_in[:, :RD], s0[2 * NB :], s1[2 * NB :], lower_inv, upper_inv,
    )


def broadcast(value, axis, root):
    mine = lax.axis_index(axis) == root
    return lax.psum(jnp.where(mine, value, jnp.zeros_like(value)), axis)


def general(matrix, pivots, lower_inv, upper_inv):
    current = matrix
    rows_dev = current.shape[0]
    cols_dev = current.shape[1]
    panel_width = pivots.shape[1]
    prow_idx = lax.axis_index(PROW)
    pcol_idx = lax.axis_index(PCOL)
    row_pos = jnp.arange(rows_dev)
    col_pos = jnp.arange(cols_dev)
    row_done = jnp.zeros((rows_dev,), bool)
    col_done = jnp.zeros((cols_dev,), bool)
    for panel_no in range(2):
        row_done = row_done | (prow_idx == panel_no) & (row_pos < panel_width)
        col_done = col_done | (pcol_idx == panel_no) & (col_pos < panel_width)
        pivot_list = pivots[panel_no]
        owner_row = pivot_list // rows_dev
        local_row = pivot_list % rows_dev
        is_owned = owner_row == prow_idx
        on_root = prow_idx == panel_no
        old_block = broadcast(current[:panel_width], PROW, panel_no)
        pivot_data = jnp.where(is_owned[:, None], current[local_row], F32(0.0))
        new_rows = lax.psum(pivot_data, PROW)
        upper_rows = hdot(lower_inv[panel_no], new_rows)
        row_block = jnp.where(col_done[None, :], new_rows, upper_rows)
        target = jnp.where(is_owned, local_row, rows_dev)
        current = current.at[target].set(old_block, mode="drop")
        current = current.at[:panel_width].set(jnp.where(on_root, row_block, current[:panel_width]))
        lower_here = hdot(current[:, :panel_width], upper_inv[panel_no])
        lower_cols = broadcast(lower_here, PCOL, panel_no)
        rank_update = hdot(lower_cols, row_block)
        keep_mask = (~row_done)[:, None] & (~col_done)[None, :]
        current = jnp.where(keep_mask, current - rank_update, current)
        panel_mask = (pcol_idx == panel_no) & (~row_done)[:, None]
        current = current.at[:, :panel_width].set(
            jnp.where(panel_mask, lower_cols, current[:, :panel_width])
        )
    return current


def local(matrix, pivots, lower_inv, upper_inv):
    rows = jnp.arange(NB, dtype=jnp.int32)
    moves = jnp.stack([pivots[0] != rows, pivots[1] != rows + RD])
    owners = jnp.where(moves, pivots // RD, NP)
    counts = jnp.sum(owners.reshape(-1, 1) == jnp.arange(NP)[None, :], axis=0)
    fits = jnp.max(counts) <= NP
    return lax.cond(fits, fast, general, matrix, pivots, lower_inv, upper_inv)


def solution(mesh):
    grid = Mesh(mesh.devices.reshape(8, 4, 8, 2), ("z", "x", "y", "core"))
    in_specs = (P(PROW, PCOL), P(), P(), P())
    return jax.shard_map(local, mesh=grid, in_specs=in_specs, out_specs=P(PROW, PCOL), check_vma=False)
```

```python
import functools

import jax
import jax.numpy as jnp
from jax import lax
from jax.experimental import pallas as pl
from jax.experimental.layout import Layout, with_layout_constraint
from jax.experimental.pallas import tpu as pltpu
from jax.sharding import Mesh, PartitionSpec as P

HIGHEST = lax.Precision.HIGHEST
F32 = jnp.float32
BF16 = jnp.bfloat16
NB = 256
RD = 768
PROW = ("z", "x")
PCOL = ("y", "core")
NP = 32
ROW_MAJOR = Layout((0, 1))


def hdot(a, b):
    return jnp.dot(a, b, precision=HIGHEST, preferred_element_type=F32)


def iota(shape, dim):
    return lax.broadcasted_iota(jnp.int32, shape, dim)


def f(mask):
    return jnp.where(mask, F32(1.0), F32(0.0))


def sum_rows(x):
    return jnp.sum(x, axis=0, keepdims=True)


def sum_cols(x):
    return jnp.sum(x, axis=1, keepdims=True)


def owner_of(row):
    return ((row >> 8) * 171) >> 9


def slot_of(rank, g):
    return ((rank & 3) * 128 + ((rank >> 2) & 7) * 16 + g * 8 + (rank >> 5)).astype(F32)


def index_math(pr, pc):
    p0r, p1r = pr[0:1, :], pr[1:2, :]
    p0c, p1c = pc[:, 0:1], pc[:, 1:2]
    sub, lane = iota((NB, NB), 0), iota((NB, NB), 1)
    lr, lc = iota((1, NB), 1), iota((NB, 1), 0)
    m_kj = f(p0c == lane + RD)
    n_kj = f(p0c == p1r)
    m_jk = f(p0r == sub + RD)
    n_jk = f(p0r == p1c)
    p1rf, p1cf = p1r.astype(F32), p1c.astype(F32)

    def dest(p0, p1, ids, has_m, has_n, piv_m, has_mk):
        stay0 = (p0 == ids) | (has_n > 0)
        end0 = jnp.where(has_m > 0, piv_m.astype(jnp.int32), p0)
        stay1 = (p1 == ids + RD) | (has_mk > 0)
        out = []
        for stay, end in ((stay0, end0), (stay1, p1)):
            own = owner_of(end)
            out.append((jnp.where(stay, NP, own), end - own * RD))
        return out

    has_m_c, has_n_c = sum_cols(m_kj), sum_cols(n_kj)
    has_m_r, has_n_r = sum_rows(m_jk), sum_rows(n_jk)
    has_mk_r, has_nk_r = sum_rows(m_kj), sum_rows(n_kj)
    has_mk_c, has_nk_c = sum_cols(m_jk), sum_cols(n_jk)
    dest_r = dest(p0r, p1r, lr, has_m_r, has_n_r, sum_rows(m_jk * p1cf), has_mk_r)
    dest_c = dest(p0c, p1c, lc, has_m_c, has_n_c, sum_cols(m_kj * p1rf), has_mk_c)
    ranks_r, ranks_c, pos_r, pos_c = [], [], [], []
    for g in range(2):
        key_r = dest_r[g][0] * NB + lr
        key_c = dest_c[g][0] * NB + lc
        rank_r = sum_rows(f(key_c < key_r)).astype(jnp.int32)
        rank_c = sum_cols(f(key_r < key_c)).astype(jnp.int32)
        ranks_r.append(rank_r)
        ranks_c.append(rank_c)
        pos_r.append(slot_of(rank_r, g))
        pos_c.append(slot_of(rank_c, g))
    w_r = jnp.where(has_mk_r > 0, sum_rows(m_kj * pos_c[0]), pos_r[1])
    w_c = jnp.where(has_mk_c > 0, sum_cols(m_jk * pos_r[0]), pos_c[1])
    src0 = jnp.where(
        has_m_c > 0,
        sum_cols(m_kj * pos_r[1]),
        jnp.where(has_n_c > 0, sum_cols(n_kj * w_r), pos_c[0]),
    )
    src1 = jnp.where(has_nk_c > 0, sum_cols(n_jk * pos_r[0]), w_c)
    rows, cols = [], []
    for g in range(2):
        rows += [ranks_r[g], dest_r[g][0], dest_r[g][1]]
        cols += [ranks_c[g], dest_c[g][0], dest_c[g][1]]
    cols += [src0.astype(jnp.int32), src1.astype(jnp.int32)]
    return rows, cols


def bdot(a, b):
    return jnp.dot(a, b, preferred_element_type=F32)


def halves(x):
    hi = x.astype(BF16)
    return hi, (x - hi.astype(F32)).astype(BF16)


def dot3(a, b):
    ah, al = halves(a)
    bh, bl = halves(b)
    return bdot(jnp.concatenate([ah, ah, al], axis=1), jnp.concatenate([bh, bl, bh], axis=0))


def pick2(p, x):
    p = p.astype(BF16)
    hi, lo = halves(x)
    return bdot(jnp.concatenate([p, p], axis=1), jnp.concatenate([hi, lo], axis=0))


def pick3(p, x):
    p = p.astype(BF16)
    hi = x.astype(BF16)
    rest = x - hi.astype(F32)
    mid = rest.astype(BF16)
    low = (rest - mid.astype(F32)).astype(BF16)
    return bdot(p, hi) + (bdot(p, mid) + bdot(p, low))


def pack_kernel(ids, pr_ref, pc_ref, a_ref, send_ref, ir_ref, ic_ref):
    me = ids[0]
    rows, cols = index_math(pr_ref[...], pc_ref[...])
    for n, v in enumerate(rows):
        ir_ref[n : n + 1, :] = v
    ir_ref[6:8, :] = jnp.zeros((2, NB), jnp.int32)
    for n, v in enumerate(cols):
        ic_ref[:, n : n + 1] = v
    line = iota((NB, NB), 0)
    rank = jnp.where(me == 1, rows[3], rows[0])
    perm = f(rank == (line >> 3) + NP * (line & 7))
    old = pick3(perm, a_ref[0:NB, :])
    line = iota((2 * NP, NB), 0)
    pick = jnp.zeros((2 * NP, RD), F32)
    for g in range(2):
        rank, own = rows[3 * g], rows[3 * g + 1]
        s = f(((line & 1) == g) & ((rank & 31) == (line >> 1)) & (own == me))
        t = f(cols[3 * g + 2] == iota((NB, RD), 1))
        pick = pick + bdot(s.astype(BF16), t.astype(BF16))
    ext = pick3(pick, a_ref[...])
    for m in range(NP):
        send_ref[m, 0:8, :] = old[8 * m : 8 * m + 8]
        send_ref[m, 8:10, :] = ext[2 * m : 2 * m + 2]


def turn_kernel(ids, ir_ref, ic_ref, ext_ref, old0_ref, old1_ref, send_ref):
    me = ids[0]
    line = iota((16, NB), 0)
    want = me + NP * (line & 7)
    own = jnp.zeros((16, 1), F32)
    for g in range(2):
        hit = f((ir_ref[3 * g : 3 * g + 1, :] == want) & ((line >> 3) == g))
        own = own + sum_cols(hit * ir_ref[3 * g + 1 : 3 * g + 2, :].astype(F32))
    own = own.astype(jnp.int32)
    old = jnp.concatenate([old0_ref[...], old1_ref[...]], axis=0)
    lane = iota((16, 2 * NP), 1)
    pick = f((own == (lane >> 1)) & ((iota((16, 2 * NP), 0) >> 3) == (lane & 1)))
    slots = jnp.where(own == NP, old, pick3(pick, ext_ref[...]))
    want = me + NP * (iota((NB, 16), 1) & 7)
    own = jnp.zeros((1, 16), F32)
    for g in range(2):
        hit = f((ic_ref[:, 3 * g : 3 * g + 1] == want) & ((iota((NB, 16), 1) >> 3) == g))
        own = own + sum_rows(hit * ic_ref[:, 3 * g + 1 : 3 * g + 2].astype(F32))
    own = own.astype(jnp.int32)
    line = iota((2 * NP, 16), 0)
    give = f((own == (line >> 1)) & ((iota((2 * NP, 16), 1) >> 3) == (line & 1)))
    back = pick3(give, old)
    for z in range(8):
        send_ref[z, 0:16, :] = slots
        send_ref[z, 16:24, :] = back[8 * z : 8 * z + 8]


def arrange(get, out_ref):
    for x in range(4):
        for z in range(8):
            out_ref[x, 16 * z : 16 * z + 16, :] = get(z, 0, 16)
            out_ref[x, 128 + 2 * z : 130 + 2 * z, :] = get(z, 16 + 2 * x, 18 + 2 * x)


def mid_kernel(in_ref, out_ref, side_ref):
    arrange(lambda z, a, b: in_ref[z, a:b, :], out_ref)
    for z in range(8):
        side_ref[24 * z : 24 * z + 24, :] = in_ref[z, :, 0:NB]


def side_kernel(ids, *refs):
    own, out, sums = refs[0], refs[8], refs[9]
    total = jnp.where(ids[2] == 0, own[...], F32(0.0))
    for r in refs[1:8]:
        total = total + r[...]
    sums[...] = total
    arrange(lambda z, a, b: sums[24 * z + a : 24 * z + b, :], out)


def slots_of(ref):
    return jnp.concatenate([ref[x, 0:128, :] for x in range(4)], axis=0)


def back_of(ref):
    return jnp.concatenate([ref[x, 128:144, :] for x in range(4)], axis=0)


def main_kernel(ids, ir_ref, ic_ref, a_ref, x_ref, li_ref, base_ref, put_ref, new0_ref, new1_ref, u0_ref):
    me = ids[0]
    put = jnp.zeros((RD, 2 * NP), F32)
    lane = iota((NB, 2 * NP), 1)
    m = ((lane >> 1) & 7) * 4 + (lane >> 4)
    for g in range(2):
        own, loc = ir_ref[3 * g + 1 : 3 * g + 2, :], ir_ref[3 * g + 2 : 3 * g + 3, :]
        t = f((own == me) & (loc == iota((RD, NB), 0)))
        s = f(((ic_ref[:, 3 * g : 3 * g + 1] & 31) == m) & ((lane & 1) == g))
        put = put + bdot(t.astype(BF16), s.astype(BF16))
    put_ref[...] = put
    x = slots_of(x_ref)
    new = []
    for n in range(2):
        new.append(pick3(f(ic_ref[:, 6 + n : 7 + n] == iota((NB, 2 * NB), 1)), x))
    new0_ref[...], new1_ref[...] = new
    u0_ref[...] = dot3(li_ref[0], new[0])
    back = back_of(x_ref)
    for r in range(3):
        part = put[NB * r : NB * r + NB]
        rows = pl.ds(NB * r, NB)
        base_ref[rows, :] = jnp.where(sum_cols(part) > 0, pick3(part, back), a_ref[rows, :])


def final_kernel(
    ids, ic_ref, raw_ref, mine_ref, there_ref, base_ref, put_ref, new0_ref, new1_ref, u0_ref,
    li_ref, ui_ref, out_ref, low_ref, up_ref,
):
    me, col, core = ids[0], ids[1], ids[3]
    mine, there = mine_ref[...], there_ref[...]
    s0 = jnp.where(core == 0, mine, there)
    s1 = jnp.where(core == 0, there, mine)
    slots0, slots1 = slots_of(s0), slots_of(s1)
    back0, back1 = back_of(s0), back_of(s1)
    perm0 = f(ic_ref[:, 6:7] == iota((NB, 2 * NB), 1))
    perm1 = f(ic_ref[:, 7:8] == iota((NB, 2 * NB), 1))
    u0 = u0_ref[...]
    u0c1 = dot3(li_ref[0], pick2(perm0, slots1))
    diag = dot3(pick2(perm1, slots0), ui_ref[0])
    next1 = new1_ref[...] - dot3(diag, u0)
    u1 = dot3(li_ref[1], next1)
    for n, u in enumerate((u0, u1)):
        hi, lo = halves(u)
        for k, v in enumerate((hi, lo, hi)):
            up_ref[NB * (3 * n + k) : NB * (3 * n + k + 1), :] = v
    raw0 = jnp.concatenate([raw_ref[y, 0] for y in range(8)], axis=0)
    raw1 = jnp.concatenate([raw_ref[y, 1] for y in range(8)], axis=0)
    for r in range(3):
        rows = pl.ds(NB * r, NB)
        part = put_ref[rows, :]
        moved = sum_cols(part) > 0
        c0 = jnp.where(moved, pick2(part, back0), raw0[NB * r : NB * r + NB])
        c1 = jnp.where(moved, pick2(part, back1), raw1[NB * r : NB * r + NB])
        low0 = dot3(c0, ui_ref[0])
        low1 = dot3(c1 - dot3(low0, u0c1), ui_ref[1])
        for n, low in enumerate((low0, low1)):
            hi, lo = halves(low)
            for k, v in enumerate((hi, hi, lo)):
                low_ref[:, NB * (3 * n + k) : NB * (3 * n + k + 1)] = v
        out_ref[rows, :] = base_ref[rows, :] - bdot(low_ref[...], up_ref[...])

        @pl.when(col == 0)
        def _():
            out_ref[rows, 0:NB] = low0

        @pl.when(col == 1)
        def _():
            out_ref[rows, 0:NB] = low1

    @pl.when(me == 0)
    def _():
        out_ref[0:NB, :] = u0

        @pl.when(col == 0)
        def _():
            out_ref[0:NB, 0:NB] = new0_ref[:, 0:NB]

    @pl.when(me == 1)
    def _():
        out_ref[0:NB, :] = u1

        @pl.when(col == 0)
        def _():
            out_ref[0:NB, 0:NB] = diag

        @pl.when(col == 1)
        def _():
            out_ref[0:NB, 0:NB] = next1[:, 0:NB]


def call(kernel, outs, ids, *args, scratch=(), flops=0):
    vmem = pl.BlockSpec(memory_space=pltpu.VMEM)
    smem = [] if ids is None else [pl.BlockSpec(memory_space=pltpu.SMEM)]
    sizes = [4 * o.size for o in jax.tree.leaves((outs, args))]
    return pl.pallas_call(
        kernel,
        out_shape=outs,
        in_specs=smem + [vmem] * len(args),
        out_specs=jax.tree.map(lambda _: vmem, outs),
        scratch_shapes=scratch,
        compiler_params=pltpu.CompilerParams(vmem_limit_bytes=40 * 1024 * 1024),
        cost_estimate=pl.CostEstimate(flops=flops, bytes_accessed=sum(sizes), transcendentals=0),
    )(*([] if ids is None else [ids]), *args)


def shape(*dims, dtype=F32):
    return jax.ShapeDtypeStruct(dims, dtype)


AROUND = (4, 3, 5, 2, 6, 1, 7)


def fast(matrix, pivots, lower_inv, upper_inv):
    prow_idx = lax.axis_index(PROW).astype(jnp.int32)
    pcol_idx = lax.axis_index(PCOL).astype(jnp.int32)
    y_idx, core_idx = lax.axis_index("y"), lax.axis_index("core")
    ids = jnp.stack([prow_idx, pcol_idx, y_idx, core_idx]).astype(jnp.int32)
    rows, ir, ic = call(
        pack_kernel,
        (shape(NP, 10, RD), shape(8, NB, dtype=jnp.int32), shape(NB, 8, dtype=jnp.int32)),
        ids, pivots, pivots.T, matrix, flops=2 * 10**9,
    )
    part = RD // 8
    panel, rows = lax.optimization_barrier((matrix[:, :NB], rows))
    piece = jnp.where(y_idx == 0, panel[:part], F32(0.0))
    for k in AROUND:
        piece = piece + lax.ppermute(panel[part * k : part * (k + 1)], "y", [(0, k)])
    raw = lax.all_gather(piece, PCOL, tiled=True).reshape(8, 2, part, NB)
    rows_in = lax.all_to_all(rows.reshape(NP, 5, 2, RD), PROW, 0, 0)
    old_in = rows_in[:2, :4].reshape(2, 8, RD)
    ext_in = rows_in[:, 4].reshape(2 * NP, RD)
    send = call(
        turn_kernel, shape(8, 24, RD), ids, ir, ic, ext_in, old_in[0], old_in[1], flops=10**8
    )
    main_z = lax.all_to_all(send, "z", 0, 0)
    main_send, side = call(mid_kernel, (shape(4, 144, RD), shape(192, NB)), None, main_z)
    main_x = lax.all_to_all(main_send, "x", 0, 0)
    parts = [lax.ppermute(side, "y", [(0, k)]) for k in AROUND]
    side_send = call(
        side_kernel, shape(4, 144, NB), ids, side, *parts, scratch=[pltpu.VMEM((192, NB), F32)]
    )
    side_send, main_x, raw = lax.optimization_barrier((side_send, main_x, raw))
    mine = lax.all_to_all(side_send, "x", 0, 0)
    base, put, new0, new1, u0 = call(
        main_kernel,
        (shape(RD, RD), shape(RD, 2 * NP), shape(NB, RD), shape(NB, RD), shape(NB, RD)),
        ids, ir, ic, matrix, main_x, lower_inv, flops=5 * 10**9,
    )
    there = lax.ppermute(mine, "core", [(0, 1), (1, 0)])
    return call(
        final_kernel, shape(RD, RD), ids, ic, raw, mine, there, base, put, new0, new1, u0,
        lower_inv, upper_inv, scratch=[pltpu.VMEM((NB, 6 * NB), BF16), pltpu.VMEM((6 * NB, RD), BF16)],
        flops=6 * 10**9,
    )


def broadcast(value, axis, root):
    mine = lax.axis_index(axis) == root
    return lax.psum(jnp.where(mine, value, jnp.zeros_like(value)), axis)


def general(matrix, pivots, lower_inv, upper_inv):
    current = matrix
    rows_dev = current.shape[0]
    cols_dev = current.shape[1]
    panel_width = pivots.shape[1]
    prow_idx = lax.axis_index(PROW)
    pcol_idx = lax.axis_index(PCOL)
    row_pos = jnp.arange(rows_dev)
    col_pos = jnp.arange(cols_dev)
    row_done = jnp.zeros((rows_dev,), bool)
    col_done = jnp.zeros((cols_dev,), bool)
    for panel_no in range(2):
        row_done = row_done | (prow_idx == panel_no) & (row_pos < panel_width)
        col_done = col_done | (pcol_idx == panel_no) & (col_pos < panel_width)
        pivot_list = pivots[panel_no]
        owner_row = pivot_list // rows_dev
        local_row = pivot_list % rows_dev
        is_owned = owner_row == prow_idx
        on_root = prow_idx == panel_no
        old_block = broadcast(current[:panel_width], PROW, panel_no)
        pivot_data = jnp.where(is_owned[:, None], current[local_row], F32(0.0))
        new_rows = lax.psum(pivot_data, PROW)
        upper_rows = hdot(lower_inv[panel_no], new_rows)
        row_block = jnp.where(col_done[None, :], new_rows, upper_rows)
        target = jnp.where(is_owned, local_row, rows_dev)
        current = current.at[target].set(old_block, mode="drop")
        current = current.at[:panel_width].set(jnp.where(on_root, row_block, current[:panel_width]))
        lower_here = hdot(current[:, :panel_width], upper_inv[panel_no])
        lower_cols = broadcast(lower_here, PCOL, panel_no)
        rank_update = hdot(lower_cols, row_block)
        keep_mask = (~row_done)[:, None] & (~col_done)[None, :]
        current = jnp.where(keep_mask, current - rank_update, current)
        panel_mask = (pcol_idx == panel_no) & (~row_done)[:, None]
        current = current.at[:, :panel_width].set(
            jnp.where(panel_mask, lower_cols, current[:, :panel_width])
        )
    return current


def local(matrix, pivots, lower_inv, upper_inv):
    rows = jnp.arange(NB, dtype=jnp.int32)
    moves = jnp.stack([pivots[0] != rows, pivots[1] != rows + RD])
    owners = jnp.where(moves, pivots // RD, NP)
    counts = jnp.sum(owners.reshape(-1, 1) == jnp.arange(NP)[None, :], axis=0)
    fits = jnp.max(counts) <= NP
    def body(state):
        out = general(with_layout_constraint(matrix, ROW_MAJOR), pivots, lower_inv, upper_inv)
        return jnp.zeros((), bool), with_layout_constraint(out, ROW_MAJOR)

    quick = fast(matrix, pivots, lower_inv, upper_inv)
    return lax.while_loop(lambda state: state[0], body, (~fits, quick))[1]


def solution(mesh):
    grid = Mesh(mesh.devices.reshape(8, 4, 8, 2), ("z", "x", "y", "core"))
    in_specs = (P(PROW, PCOL), P(), P(), P())
    return jax.shard_map(local, mesh=grid, in_specs=in_specs, out_specs=P(PROW, PCOL), check_vma=False)
```

```python
import functools

import jax
import jax.numpy as jnp
from jax import lax
from jax.experimental import pallas as pl
from jax.experimental.layout import Layout, with_layout_constraint
from jax.experimental.pallas import tpu as pltpu
from jax.sharding import Mesh, PartitionSpec as P

HIGHEST = lax.Precision.HIGHEST
F32 = jnp.float32
BF16 = jnp.bfloat16
NB = 256
RD = 768
PROW = ("z", "x")
PCOL = ("y", "core")
NP = 32
ROW_MAJOR = Layout((0, 1))


def hdot(a, b):
    return jnp.dot(a, b, precision=HIGHEST, preferred_element_type=F32)


def iota(shape, dim):
    return lax.broadcasted_iota(jnp.int32, shape, dim)


def f(mask):
    return jnp.where(mask, F32(1.0), F32(0.0))


def sum_rows(x):
    return jnp.sum(x, axis=0, keepdims=True)


def sum_cols(x):
    return jnp.sum(x, axis=1, keepdims=True)


def owner_of(row):
    return ((row >> 8) * 171) >> 9


def slot_of(rank, g):
    return ((rank & 3) * 128 + ((rank >> 2) & 7) * 16 + g * 8 + (rank >> 5)).astype(F32)


def index_math(pr, pc):
    p0r, p1r = pr[0:1, :], pr[1:2, :]
    p0c, p1c = pc
    sub, lane = iota((NB, NB), 0), iota((NB, NB), 1)
    lr, lc = iota((1, NB), 1), iota((NB, 1), 0)
    m_kj = f(p0c == lane + RD)
    n_kj = f(p0c == p1r)
    m_jk = f(p0r == sub + RD)
    n_jk = f(p0r == p1c)
    p1rf, p1cf = p1r.astype(F32), p1c.astype(F32)

    def dest(p0, p1, ids, has_m, has_n, piv_m, has_mk):
        stay0 = (p0 == ids) | (has_n > 0)
        end0 = jnp.where(has_m > 0, piv_m.astype(jnp.int32), p0)
        stay1 = (p1 == ids + RD) | (has_mk > 0)
        out = []
        for stay, end in ((stay0, end0), (stay1, p1)):
            own = owner_of(end)
            out.append((jnp.where(stay, NP, own), end - own * RD))
        return out

    has_m_c, has_n_c = sum_cols(m_kj), sum_cols(n_kj)
    has_m_r, has_n_r = sum_rows(m_jk), sum_rows(n_jk)
    has_mk_r, has_nk_r = sum_rows(m_kj), sum_rows(n_kj)
    has_mk_c, has_nk_c = sum_cols(m_jk), sum_cols(n_jk)
    dest_r = dest(p0r, p1r, lr, has_m_r, has_n_r, sum_rows(m_jk * p1cf), has_mk_r)
    dest_c = dest(p0c, p1c, lc, has_m_c, has_n_c, sum_cols(m_kj * p1rf), has_mk_c)
    ranks_r, ranks_c, pos_r, pos_c = [], [], [], []
    for g in range(2):
        key_r = dest_r[g][0] * NB + lr
        key_c = dest_c[g][0] * NB + lc
        rank_r = sum_rows(f(key_c < key_r)).astype(jnp.int32)
        rank_c = sum_cols(f(key_r < key_c)).astype(jnp.int32)
        ranks_r.append(rank_r)
        ranks_c.append(rank_c)
        pos_r.append(slot_of(rank_r, g))
        pos_c.append(slot_of(rank_c, g))
    w_r = jnp.where(has_mk_r > 0, sum_rows(m_kj * pos_c[0]), pos_r[1])
    w_c = jnp.where(has_mk_c > 0, sum_cols(m_jk * pos_r[0]), pos_c[1])
    src0 = jnp.where(
        has_m_c > 0,
        sum_cols(m_kj * pos_r[1]),
        jnp.where(has_n_c > 0, sum_cols(n_kj * w_r), pos_c[0]),
    )
    src1 = jnp.where(has_nk_c > 0, sum_cols(n_jk * pos_r[0]), w_c)
    rows, cols = [], []
    for g in range(2):
        rows += [ranks_r[g], dest_r[g][0], dest_r[g][1]]
        cols += [ranks_c[g], dest_c[g][0], dest_c[g][1]]
    cols += [src0.astype(jnp.int32), src1.astype(jnp.int32)]
    return rows, cols


def bdot(a, b):
    return jnp.dot(a, b, preferred_element_type=F32)


def halves(x):
    hi = x.astype(BF16)
    return hi, (x - hi.astype(F32)).astype(BF16)


def dot3(a, b):
    ah, al = halves(a)
    bh, bl = halves(b)
    return bdot(jnp.concatenate([ah, ah, al], axis=1), jnp.concatenate([bh, bl, bh], axis=0))


def pick2(p, x):
    p = p.astype(BF16)
    hi, lo = halves(x)
    return bdot(jnp.concatenate([p, p], axis=1), jnp.concatenate([hi, lo], axis=0))


def pick3(p, x):
    p = p.astype(BF16)
    hi = x.astype(BF16)
    rest = x - hi.astype(F32)
    mid = rest.astype(BF16)
    low = (rest - mid.astype(F32)).astype(BF16)
    return bdot(p, hi) + (bdot(p, mid) + bdot(p, low))


def pack_kernel(ids, p_ref, a_ref, send_ref, ir_ref, ic_ref, most_ref, *piece_refs):
    me = ids[0]
    for n, r in enumerate(piece_refs):
        rows_n = r.shape[0]
        r[...] = a_ref[rows_n * n : rows_n * (n + 1), 0:NB]
    pr = p_ref[...]
    eye = iota((NB, NB), 0) == iota((NB, NB), 1)
    turned = [sum_cols(jnp.where(eye, pr[n : n + 1, :].astype(F32), F32(0.0))) for n in range(2)]
    rows, cols = index_math(pr, [t.astype(jnp.int32) for t in turned])
    for n, v in enumerate(rows):
        ir_ref[n : n + 1, :] = v
    ir_ref[6:8, :] = jnp.zeros((2, NB), jnp.int32)
    for n, v in enumerate(cols):
        ic_ref[:, n : n + 1] = v
    counts = [sum_rows(f(cols[3 * g + 1] == iota((NB, NP), 1))) for g in range(2)]
    most_ref[0] = jnp.max(jnp.maximum(counts[0], counts[1])).astype(jnp.int32)
    line = iota((NB, NB), 0)
    rank = jnp.where(me == 1, rows[3], rows[0])
    perm = f(rank == (line >> 3) + NP * (line & 7))
    old = pick3(perm, a_ref[0:NB, :])
    line = iota((2 * NP, NB), 0)
    pick = jnp.zeros((2 * NP, RD), F32)
    for g in range(2):
        rank, own = rows[3 * g], rows[3 * g + 1]
        s = f(((line & 1) == g) & ((rank & 31) == (line >> 1)) & (own == me))
        t = f(cols[3 * g + 2] == iota((NB, RD), 1))
        pick = pick + bdot(s.astype(BF16), t.astype(BF16))
    ext = pick3(pick, a_ref[...])
    for m in range(NP):
        for q in range(4):
            send_ref[m, q] = old[8 * m + 2 * q : 8 * m + 2 * q + 2]
        send_ref[m, 4] = ext[2 * m : 2 * m + 2]


def turn_kernel(ids, ir_ref, ic_ref, in_ref, send_ref, side_ref, old_ref, ext_ref):
    me = ids[0]
    for q in range(4):
        old_ref[2 * q : 2 * q + 2, :] = in_ref[0, q]
        old_ref[8 + 2 * q : 10 + 2 * q, :] = in_ref[1, q]
    for m in range(NP):
        ext_ref[2 * m : 2 * m + 2, :] = in_ref[m, 4]
    line = iota((16, NB), 0)
    want = me + NP * (line & 7)
    own = jnp.zeros((16, 1), F32)
    for g in range(2):
        hit = f((ir_ref[3 * g : 3 * g + 1, :] == want) & ((line >> 3) == g))
        own = own + sum_cols(hit * ir_ref[3 * g + 1 : 3 * g + 2, :].astype(F32))
    own = own.astype(jnp.int32)
    old = old_ref[...]
    lane = iota((16, 2 * NP), 1)
    pick = f((own == (lane >> 1)) & ((iota((16, 2 * NP), 0) >> 3) == (lane & 1)))
    slots = jnp.where(own == NP, old, pick3(pick, ext_ref[...]))
    want = me + NP * (iota((NB, 16), 1) & 7)
    own = jnp.zeros((1, 16), F32)
    for g in range(2):
        hit = f((ic_ref[:, 3 * g : 3 * g + 1] == want) & ((iota((NB, 16), 1) >> 3) == g))
        own = own + sum_rows(hit * ic_ref[:, 3 * g + 1 : 3 * g + 2].astype(F32))
    own = own.astype(jnp.int32)
    line = iota((2 * NP, 16), 0)
    give = f((own == (line >> 1)) & ((iota((2 * NP, 16), 1) >> 3) == (line & 1)))
    back = pick3(give, old)
    for z in range(8):
        send_ref[z, 0:16, :] = slots
        send_ref[z, 16:24, :] = back[8 * z : 8 * z + 8]
    side_ref[0:16, :] = slots[:, 0:NB]
    side_ref[16:80, :] = back[:, 0:NB]


def side_kernel(ids, *refs):
    own, out, sums = refs[0], refs[8], refs[9]
    total = jnp.where(ids[2] == 0, own[...], F32(0.0))
    for r in refs[1:8]:
        total = total + r[...]
    sums[...] = total
    for m in range(NP):
        for h in range(2):
            cut = slice(128 * h, 128 * h + 128)
            out[m, 16 * h : 16 * h + 16, :] = sums[0:16, cut]
            out[m, 32 + 2 * h : 34 + 2 * h, :] = sums[16 + 2 * m : 18 + 2 * m, cut]
        out[m, 36:40, :] = jnp.zeros((4, 128), F32)


def mid_kernel(ids, in_ref, *out_refs):
    for s, out_ref in enumerate(out_refs):
        to = (ids[0] + s) & 3
        for z in range(8):
            out_ref[16 * z : 16 * z + 16, :] = in_ref[z, 0:16, :]
            back = in_ref[z, 16:18, :]
            for x in range(1, 4):
                back = jnp.where(to == x, in_ref[z, 16 + 2 * x : 18 + 2 * x, :], back)
            out_ref[128 + 2 * z : 130 + 2 * z, :] = back


def pre_kernel(raw_ref, ui_ref, low0_ref, end1_ref):
    for n, out in enumerate((low0_ref, end1_ref)):
        raw = jnp.concatenate([raw_ref[y, n] for y in range(8)], axis=0)
        out[...] = dot3(raw, ui_ref[n])


def main_kernel(
    ids, ir_ref, ic_ref, a_ref, x0_ref, x1_ref, x2_ref, x3_ref, low0_ref, li_ref,
    base_ref, put_ref, back_ref, new0_ref, new1_ref, u0_ref,
):
    me = ids[0]
    put = jnp.zeros((RD, 2 * NP), F32)
    lane = iota((NB, 2 * NP), 1)
    m = ((lane >> 1) & 7) * 4 + (lane >> 4)
    for g in range(2):
        own, loc = ir_ref[3 * g + 1 : 3 * g + 2, :], ir_ref[3 * g + 2 : 3 * g + 3, :]
        t = f((own == me) & (loc == iota((RD, NB), 0)))
        s = f(((ic_ref[:, 3 * g : 3 * g + 1] & 31) == m) & ((lane & 1) == g))
        put = put + bdot(t.astype(BF16), s.astype(BF16))
    put_ref[...] = put
    blocks = (x0_ref, x1_ref, x2_ref, x3_ref)
    slots = jnp.concatenate([r[0:128, :] for r in blocks], axis=0)
    for x in range(4):
        s = (me - x) & 3
        back = blocks[0][128:144, :]
        for k in range(1, 4):
            back = jnp.where(s == k, blocks[k][128:144, :], back)
        back_ref[16 * x : 16 * x + 16, :] = back
    lane = iota((NB, 2 * NB), 1)
    slot = ((me - (lane >> 7)) & 3) * 128 + (lane & 127)
    new0 = pick3(f(ic_ref[:, 6:7] == slot), slots)
    new1_ref[...] = pick3(f(ic_ref[:, 7:8] == slot), slots)
    new0_ref[...] = new0[:, 0:NB]
    u0 = dot3(li_ref[0], new0)
    u0_ref[...] = u0
    for r in range(3):
        rows = pl.ds(NB * r, NB)
        base_ref[rows, :] = a_ref[rows, :] - dot3(low0_ref[rows, :], u0)


def final_kernel(
    ids, ic_ref, mine_ref, there_ref, base_ref, put_ref, back_ref, new0_ref, new1_ref, u0_ref,
    low0_ref, end1_ref, li_ref, ui_ref, out_ref, slots_ref, rows_ref,
):
    me, col, core = ids[0], ids[1], ids[3]
    for x in range(4):
        for z in range(8):
            m, n = 4 * z + x, 8 * x + z
            mine, there = mine_ref[m], there_ref[m]
            for k in range(2):
                got = jnp.where(core == k, mine, there)
                for h in range(2):
                    cut = slice(128 * h, 128 * h + 128)
                    slots_ref[k, 16 * n : 16 * n + 16, cut] = got[16 * h : 16 * h + 16]
                    rows_ref[k, 2 * n : 2 * n + 2, cut] = got[32 + 2 * h : 34 + 2 * h]
    u0 = u0_ref[...]
    perm0 = f(ic_ref[:, 6:7] == iota((NB, 2 * NB), 1))
    perm1 = f(ic_ref[:, 7:8] == iota((NB, 2 * NB), 1))
    diag = dot3(pick2(perm1, slots_ref[0]), ui_ref[0])
    next1 = new1_ref[...] - dot3(diag, u0)
    u1 = dot3(li_ref[1], next1)
    fill = dot3(dot3(li_ref[0], pick2(perm0, slots_ref[1])), ui_ref[1])
    low0_back = dot3(rows_ref[0], ui_ref[0])
    low1_back = dot3(rows_ref[1], ui_ref[1]) - dot3(low0_back, fill)
    back = back_ref[...] - dot3(low0_back, u0) - dot3(low1_back, u1)
    for r in range(3):
        rows = pl.ds(NB * r, NB)
        put = put_ref[rows, :]
        moved = sum_cols(put) > 0
        low0 = low0_ref[rows, :]
        low1 = end1_ref[rows, :] - dot3(low0, fill)
        out_ref[rows, :] = jnp.where(moved, pick2(put, back), base_ref[rows, :] - dot3(low1, u1))

        @pl.when(col == 0)
        def _():
            out_ref[rows, 0:NB] = jnp.where(moved, pick2(put, low0_back), low0)

        @pl.when(col == 1)
        def _():
            out_ref[rows, 0:NB] = jnp.where(moved, pick2(put, low1_back), low1)

    @pl.when(me == 0)
    def _():
        out_ref[0:NB, :] = u0

        @pl.when(col == 0)
        def _():
            out_ref[0:NB, 0:NB] = new0_ref[...]

    @pl.when(me == 1)
    def _():
        out_ref[0:NB, :] = u1

        @pl.when(col == 0)
        def _():
            out_ref[0:NB, 0:NB] = diag

        @pl.when(col == 1)
        def _():
            out_ref[0:NB, 0:NB] = next1[:, 0:NB]


SCALAR = pl.BlockSpec(memory_space=pltpu.SMEM)


def call(kernel, outs, ids, *args, scratch=(), flops=0):
    vmem = pl.BlockSpec(memory_space=pltpu.VMEM)
    smem = [] if ids is None else [SCALAR]
    sizes = [4 * o.size for o in jax.tree.leaves((outs, args))]
    return pl.pallas_call(
        kernel,
        out_shape=outs,
        in_specs=smem + [vmem] * len(args),
        out_specs=jax.tree.map(lambda o: SCALAR if o.shape == (1,) else vmem, outs),
        scratch_shapes=scratch,
        compiler_params=pltpu.CompilerParams(vmem_limit_bytes=40 * 1024 * 1024),
        cost_estimate=pl.CostEstimate(flops=flops, bytes_accessed=min(sizes), transcendentals=0),
    )(*([] if ids is None else [ids]), *args)


def shape(*dims, dtype=F32):
    return jax.ShapeDtypeStruct(dims, dtype)


AROUND = (4, 3, 5, 2, 6, 1, 7)


def fast(matrix, pivots, lower_inv, upper_inv):
    prow_idx = lax.axis_index(PROW).astype(jnp.int32)
    pcol_idx = lax.axis_index(PCOL).astype(jnp.int32)
    y_idx, core_idx = lax.axis_index("y"), lax.axis_index("core")
    ids = jnp.stack([prow_idx, pcol_idx, y_idx, core_idx]).astype(jnp.int32)
    part = RD // 8
    rows, ir, ic, most, *panel = call(
        pack_kernel,
        (
            shape(NP, 5, 2, RD), shape(8, NB, dtype=jnp.int32), shape(NB, 8, dtype=jnp.int32),
            shape(1, dtype=jnp.int32), *[shape(part, NB)] * 8,
        ),
        ids, pivots, matrix, flops=10**6,
    )
    rows_in = lax.all_to_all(rows, PROW, 0, 0)
    piece = jnp.where(y_idx == 0, panel[0], F32(0.0))
    for k in AROUND:
        piece = piece + lax.ppermute(panel[k], "y", [(0, k)])
    rows_in, piece = lax.optimization_barrier((rows_in, piece))
    raw = lax.all_gather(piece, PCOL, tiled=True).reshape(8, 2, part, NB)
    send, side = call(
        turn_kernel, (shape(8, 24, RD), shape(80, NB)), ids, ir, ic, rows_in,
        scratch=[pltpu.VMEM((16, RD), F32), pltpu.VMEM((2 * NP, RD), F32)], flops=10**6,
    )
    main_z = lax.all_to_all(send, "z", 0, 0)
    parts = [lax.ppermute(side, "y", [(0, k)]) for k in AROUND]
    side_send = call(
        side_kernel, shape(NP, 40, 128), ids, side, *parts, scratch=[pltpu.VMEM((80, NB), F32)]
    )
    main_send = call(mid_kernel, [shape(144, RD)] * 4, ids, main_z)
    side_send, main_send = lax.optimization_barrier((side_send, main_send))
    mine = lax.all_to_all(side_send, PROW, 0, 0)
    main_x = [main_send[0]] + [
        lax.ppermute(main_send[k], "x", [(i, (i + k) % 4) for i in range(4)]) for k in range(1, 4)
    ]
    mine, main_x, raw = lax.optimization_barrier((mine, main_x, raw))
    low0, end1 = call(pre_kernel, (shape(RD, NB), shape(RD, NB)), None, raw, upper_inv, flops=10**6)
    base, put, back, new0, new1, u0 = call(
        main_kernel,
        (
            shape(RD, RD), shape(RD, 2 * NP), shape(2 * NP, RD), shape(NB, NB), shape(NB, RD),
            shape(NB, RD),
        ),
        ids, ir, ic, matrix, *main_x, low0, lower_inv, flops=10**6,
    )
    there = lax.ppermute(mine, "core", [(0, 1), (1, 0)])
    out = call(
        final_kernel, shape(RD, RD), ids, ic, mine, there, base, put, back, new0, new1, u0,
        low0, end1, lower_inv, upper_inv,
        scratch=[pltpu.VMEM((2, 2 * NB, NB), F32), pltpu.VMEM((2, 2 * NP, NB), F32)],
        flops=10**6,
    )
    return out, most[0]


def broadcast(value, axis, root):
    mine = lax.axis_index(axis) == root
    return lax.psum(jnp.where(mine, value, jnp.zeros_like(value)), axis)


def general(matrix, pivots, lower_inv, upper_inv):
    current = matrix
    rows_dev = current.shape[0]
    cols_dev = current.shape[1]
    panel_width = pivots.shape[1]
    prow_idx = lax.axis_index(PROW)
    pcol_idx = lax.axis_index(PCOL)
    row_pos = jnp.arange(rows_dev)
    col_pos = jnp.arange(cols_dev)
    row_done = jnp.zeros((rows_dev,), bool)
    col_done = jnp.zeros((cols_dev,), bool)
    for panel_no in range(2):
        row_done = row_done | (prow_idx == panel_no) & (row_pos < panel_width)
        col_done = col_done | (pcol_idx == panel_no) & (col_pos < panel_width)
        pivot_list = pivots[panel_no]
        owner_row = pivot_list // rows_dev
        local_row = pivot_list % rows_dev
        is_owned = owner_row == prow_idx
        on_root = prow_idx == panel_no
        old_block = broadcast(current[:panel_width], PROW, panel_no)
        pivot_data = jnp.where(is_owned[:, None], current[local_row], F32(0.0))
        new_rows = lax.psum(pivot_data, PROW)
        upper_rows = hdot(lower_inv[panel_no], new_rows)
        row_block = jnp.where(col_done[None, :], new_rows, upper_rows)
        target = jnp.where(is_owned, local_row, rows_dev)
        current = current.at[target].set(old_block, mode="drop")
        current = current.at[:panel_width].set(jnp.where(on_root, row_block, current[:panel_width]))
        lower_here = hdot(current[:, :panel_width], upper_inv[panel_no])
        lower_cols = broadcast(lower_here, PCOL, panel_no)
        rank_update = hdot(lower_cols, row_block)
        keep_mask = (~row_done)[:, None] & (~col_done)[None, :]
        current = jnp.where(keep_mask, current - rank_update, current)
        panel_mask = (pcol_idx == panel_no) & (~row_done)[:, None]
        current = current.at[:, :panel_width].set(
            jnp.where(panel_mask, lower_cols, current[:, :panel_width])
        )
    return current


def local(matrix, pivots, lower_inv, upper_inv):
    def body(state):
        out = general(with_layout_constraint(matrix, ROW_MAJOR), pivots, lower_inv, upper_inv)
        return jnp.zeros((), bool), with_layout_constraint(out, ROW_MAJOR)

    quick, most = fast(matrix, pivots, lower_inv, upper_inv)
    return lax.while_loop(lambda state: state[0], body, (most > NP, quick))[1]


def solution(mesh):
    grid = Mesh(mesh.devices.reshape(8, 4, 8, 2), ("z", "x", "y", "core"))
    in_specs = (P(PROW, PCOL), P(), P(), P())
    return jax.shard_map(local, mesh=grid, in_specs=in_specs, out_specs=P(PROW, PCOL), check_vma=False)
```

```python
import functools

import jax
import jax.numpy as jnp
from jax import lax
from jax.experimental import pallas as pl
from jax.experimental.layout import Layout, with_layout_constraint
from jax.experimental.pallas import tpu as pltpu
from jax.sharding import Mesh, PartitionSpec as P

HIGHEST = lax.Precision.HIGHEST
F32 = jnp.float32
BF16 = jnp.bfloat16
NB = 256
RD = 768
PROW = ("z", "x")
PCOL = ("y", "core")
NP = 32
ROW_MAJOR = Layout((0, 1))


def hdot(a, b):
    return jnp.dot(a, b, precision=HIGHEST, preferred_element_type=F32)


def iota(shape, dim):
    return lax.broadcasted_iota(jnp.int32, shape, dim)


def f(mask):
    return jnp.where(mask, F32(1.0), F32(0.0))


def sum_rows(x):
    return jnp.sum(x, axis=0, keepdims=True)


def sum_cols(x):
    return jnp.sum(x, axis=1, keepdims=True)


def owner_of(row):
    return ((row >> 8) * 171) >> 9


def slot_of(rank, g):
    return ((rank & 3) * 128 + ((rank >> 2) & 7) * 16 + g * 8 + (rank >> 5)).astype(F32)


def index_math(pr, pc):
    p0r, p1r = pr[0:1, :], pr[1:2, :]
    p0c, p1c = pc
    sub, lane = iota((NB, NB), 0), iota((NB, NB), 1)
    lr, lc = iota((1, NB), 1), iota((NB, 1), 0)
    m_kj = f(p0c == lane + RD)
    n_kj = f(p0c == p1r)
    m_jk = f(p0r == sub + RD)
    n_jk = f(p0r == p1c)
    p1rf, p1cf = p1r.astype(F32), p1c.astype(F32)

    def dest(p0, p1, ids, has_m, has_n, piv_m, has_mk):
        stay0 = (p0 == ids) | (has_n > 0)
        end0 = jnp.where(has_m > 0, piv_m.astype(jnp.int32), p0)
        stay1 = (p1 == ids + RD) | (has_mk > 0)
        out = []
        for stay, end in ((stay0, end0), (stay1, p1)):
            own = owner_of(end)
            out.append((jnp.where(stay, NP, own), end - own * RD))
        return out

    has_m_c, has_n_c = sum_cols(m_kj), sum_cols(n_kj)
    has_m_r, has_n_r = sum_rows(m_jk), sum_rows(n_jk)
    has_mk_r, has_nk_r = sum_rows(m_kj), sum_rows(n_kj)
    has_mk_c, has_nk_c = sum_cols(m_jk), sum_cols(n_jk)
    dest_r = dest(p0r, p1r, lr, has_m_r, has_n_r, sum_rows(m_jk * p1cf), has_mk_r)
    dest_c = dest(p0c, p1c, lc, has_m_c, has_n_c, sum_cols(m_kj * p1rf), has_mk_c)
    ranks_r, ranks_c, pos_r, pos_c = [], [], [], []
    for g in range(2):
        key_r = dest_r[g][0] * NB + lr
        key_c = dest_c[g][0] * NB + lc
        rank_r = sum_rows(f(key_c < key_r)).astype(jnp.int32)
        rank_c = sum_cols(f(key_r < key_c)).astype(jnp.int32)
        ranks_r.append(rank_r)
        ranks_c.append(rank_c)
        pos_r.append(slot_of(rank_r, g))
        pos_c.append(slot_of(rank_c, g))
    w_r = jnp.where(has_mk_r > 0, sum_rows(m_kj * pos_c[0]), pos_r[1])
    w_c = jnp.where(has_mk_c > 0, sum_cols(m_jk * pos_r[0]), pos_c[1])
    src0 = jnp.where(
        has_m_c > 0,
        sum_cols(m_kj * pos_r[1]),
        jnp.where(has_n_c > 0, sum_cols(n_kj * w_r), pos_c[0]),
    )
    src1 = jnp.where(has_nk_c > 0, sum_cols(n_jk * pos_r[0]), w_c)
    rows, cols = [], []
    for g in range(2):
        rows += [ranks_r[g], dest_r[g][0], dest_r[g][1]]
        cols += [ranks_c[g], dest_c[g][0], dest_c[g][1]]
    cols += [src0.astype(jnp.int32), src1.astype(jnp.int32)]
    return rows, cols


def bdot(a, b):
    return jnp.dot(a, b, preferred_element_type=F32)


def halves(x):
    hi = x.astype(BF16)
    return hi, (x - hi.astype(F32)).astype(BF16)


def dot3(a, b):
    ah, al = halves(a)
    bh, bl = halves(b)
    return bdot(jnp.concatenate([ah, ah, al], axis=1), jnp.concatenate([bh, bl, bh], axis=0))


def pick2(p, x):
    p = p.astype(BF16)
    hi, lo = halves(x)
    return bdot(jnp.concatenate([p, p], axis=1), jnp.concatenate([hi, lo], axis=0))


def pick3(p, x):
    p = p.astype(BF16)
    hi = x.astype(BF16)
    rest = x - hi.astype(F32)
    mid = rest.astype(BF16)
    low = (rest - mid.astype(F32)).astype(BF16)
    return bdot(p, hi) + (bdot(p, mid) + bdot(p, low))


def pack_kernel(ids, p_ref, a_ref, send_ref, ir_ref, ic_ref, most_ref, *piece_refs):
    me = ids[0]
    for n, r in enumerate(piece_refs):
        rows_n = r.shape[0]
        r[...] = a_ref[rows_n * n : rows_n * (n + 1), 0:NB]
    pr = p_ref[...]
    eye = iota((NB, NB), 0) == iota((NB, NB), 1)
    turned = [sum_cols(jnp.where(eye, pr[n : n + 1, :].astype(F32), F32(0.0))) for n in range(2)]
    rows, cols = index_math(pr, [t.astype(jnp.int32) for t in turned])
    for n, v in enumerate(rows):
        ir_ref[n : n + 1, :] = v
    ir_ref[6:8, :] = jnp.zeros((2, NB), jnp.int32)
    for n, v in enumerate(cols):
        ic_ref[:, n : n + 1] = v
    counts = [sum_rows(f(cols[3 * g + 1] == iota((NB, NP), 1))) for g in range(2)]
    most_ref[0] = jnp.max(jnp.maximum(counts[0], counts[1])).astype(jnp.int32)
    line = iota((NB, NB), 0)
    rank = jnp.where(me == 1, rows[3], rows[0])
    perm = f(rank == (line >> 3) + NP * (line & 7))
    old = pick3(perm, a_ref[0:NB, :])
    line = iota((2 * NP, NB), 0)
    pick = jnp.zeros((2 * NP, RD), F32)
    for g in range(2):
        rank, own = rows[3 * g], rows[3 * g + 1]
        s = f(((line & 1) == g) & ((rank & 31) == (line >> 1)) & (own == me))
        t = f(cols[3 * g + 2] == iota((NB, RD), 1))
        pick = pick + bdot(s.astype(BF16), t.astype(BF16))
    ext = pick3(pick, a_ref[...])
    for m in range(NP):
        for q in range(4):
            send_ref[m, q] = old[8 * m + 2 * q : 8 * m + 2 * q + 2]
        send_ref[m, 4] = ext[2 * m : 2 * m + 2]


def turn_kernel(ids, ir_ref, ic_ref, in_ref, send_ref, side_ref, old_ref, ext_ref):
    me = ids[0]
    for q in range(4):
        old_ref[2 * q : 2 * q + 2, :] = in_ref[0, q]
        old_ref[8 + 2 * q : 10 + 2 * q, :] = in_ref[1, q]
    for m in range(NP):
        ext_ref[2 * m : 2 * m + 2, :] = in_ref[m, 4]
    line = iota((16, NB), 0)
    want = me + NP * (line & 7)
    own = jnp.zeros((16, 1), F32)
    for g in range(2):
        hit = f((ir_ref[3 * g : 3 * g + 1, :] == want) & ((line >> 3) == g))
        own = own + sum_cols(hit * ir_ref[3 * g + 1 : 3 * g + 2, :].astype(F32))
    own = own.astype(jnp.int32)
    old = old_ref[...]
    lane = iota((16, 2 * NP), 1)
    pick = f((own == (lane >> 1)) & ((iota((16, 2 * NP), 0) >> 3) == (lane & 1)))
    slots = jnp.where(own == NP, old, pick3(pick, ext_ref[...]))
    want = me + NP * (iota((NB, 16), 1) & 7)
    own = jnp.zeros((1, 16), F32)
    for g in range(2):
        hit = f((ic_ref[:, 3 * g : 3 * g + 1] == want) & ((iota((NB, 16), 1) >> 3) == g))
        own = own + sum_rows(hit * ic_ref[:, 3 * g + 1 : 3 * g + 2].astype(F32))
    own = own.astype(jnp.int32)
    line = iota((2 * NP, 16), 0)
    give = f((own == (line >> 1)) & ((iota((2 * NP, 16), 1) >> 3) == (line & 1)))
    back = pick3(give, old)
    for z in range(8):
        send_ref[z, 0:16, :] = slots
        send_ref[z, 16:24, :] = back[8 * z : 8 * z + 8]
    side_ref[0:16, :] = slots[:, 0:NB]
    side_ref[16:80, :] = back[:, 0:NB]


def side_kernel(ids, *refs):
    own, outs, sums = refs[0], refs[8:12], refs[12]
    total = jnp.where(ids[2] == 0, own[...], F32(0.0))
    for r in refs[1:8]:
        total = total + r[...]
    sums[...] = total
    for s, out in enumerate(outs):
        to = (ids[0] + s) & 3
        for h in range(2):
            cut = slice(128 * h, 128 * h + 128)
            out[16 * h : 16 * h + 16, :] = sums[0:16, cut]
            for z in range(8):
                back = sums[16 + 8 * z : 18 + 8 * z, cut]
                for x in range(1, 4):
                    at = 16 + 8 * z + 2 * x
                    back = jnp.where(to == x, sums[at : at + 2, cut], back)
                at = 32 + 16 * h + 2 * z
                out[at : at + 2, :] = back


def join_kernel(*refs):
    blocks, out = refs[:4], refs[4]
    for z in range(8):
        for s, block in enumerate(blocks):
            for h in range(2):
                out[z, 64 * h + 16 * s : 64 * h + 16 * s + 16, :] = block[16 * h : 16 * h + 16, :]
                at = 32 + 16 * h + 2 * z
                out[z, 128 + 8 * h + 2 * s : 130 + 8 * h + 2 * s, :] = block[at : at + 2, :]


def mid_kernel(ids, in_ref, *out_refs):
    for s, out_ref in enumerate(out_refs):
        to = (ids[0] + s) & 3
        for z in range(8):
            out_ref[16 * z : 16 * z + 16, :] = in_ref[z, 0:16, :]
            back = in_ref[z, 16:18, :]
            for x in range(1, 4):
                back = jnp.where(to == x, in_ref[z, 16 + 2 * x : 18 + 2 * x, :], back)
            out_ref[128 + 2 * z : 130 + 2 * z, :] = back


def main_kernel(
    ids, ir_ref, ic_ref, a_ref, x0_ref, x1_ref, x2_ref, x3_ref, li_ref, ui_ref, raw_ref,
    base_ref, put_ref, back_ref, new0_ref, new1_ref, u0_ref, low0_ref, end1_ref, held_ref, sem,
):
    me = ids[0]
    fetch = pltpu.make_async_copy(raw_ref, held_ref, sem)
    fetch.start()
    put = jnp.zeros((RD, 2 * NP), F32)
    lane = iota((NB, 2 * NP), 1)
    m = (lane >> 3) * 4 + ((me - ((lane >> 1) & 3)) & 3)
    for g in range(2):
        own, loc = ir_ref[3 * g + 1 : 3 * g + 2, :], ir_ref[3 * g + 2 : 3 * g + 3, :]
        t = f((own == me) & (loc == iota((RD, NB), 0)))
        s = f(((ic_ref[:, 3 * g : 3 * g + 1] & 31) == m) & ((lane & 1) == g))
        put = put + bdot(t.astype(BF16), s.astype(BF16))
    put_ref[...] = put
    blocks = (x0_ref, x1_ref, x2_ref, x3_ref)
    slots = jnp.concatenate([r[0:128, :] for r in blocks], axis=0)
    for z in range(8):
        for s in range(4):
            at = 8 * z + 2 * s
            back_ref[at : at + 2, :] = blocks[s][128 + 2 * z : 130 + 2 * z, :]
    lane = iota((NB, 2 * NB), 1)
    slot = ((me - (lane >> 7)) & 3) * 128 + (lane & 127)
    new0 = pick2(f(ic_ref[:, 6:7] == slot), slots)
    new1_ref[...] = pick2(f(ic_ref[:, 7:8] == slot), slots)
    new0_ref[...] = new0[:, 0:NB]
    u0 = dot3(li_ref[0], new0)
    u0_ref[...] = u0
    fetch.wait()
    for n, out in enumerate((low0_ref, end1_ref)):
        raw = jnp.concatenate([held_ref[y, n] for y in range(8)], axis=0)
        out[...] = dot3(raw, ui_ref[n])
    for r in range(3):
        rows = pl.ds(NB * r, NB)
        base_ref[rows, :] = a_ref[rows, :] - dot3(low0_ref[rows, :], u0)


def final_kernel(
    ids, ic_ref, mine_ref, there_ref, base_ref, put_ref, back_ref, new0_ref, new1_ref, u0_ref,
    low0_ref, end1_ref, li_ref, ui_ref, out_ref, done_ref, slots_ref, rows_ref, sem,
):
    me, col, core = ids[0], ids[1], ids[3]
    for z in range(8):
        mine, there = mine_ref[z], there_ref[z]
        for k in range(2):
            got = jnp.where(core == k, mine, there)
            for h in range(2):
                cut = slice(128 * h, 128 * h + 128)
                slots_ref[k, 64 * z : 64 * z + 64, cut] = got[64 * h : 64 * h + 64]
                rows_ref[k, 8 * z : 8 * z + 8, cut] = got[128 + 8 * h : 136 + 8 * h]
    u0 = u0_ref[...]
    lane = iota((NB, 2 * NB), 1)
    slot = ((me - (lane >> 4)) & 3) * 128 + (lane >> 6) * 16 + (lane & 15)
    diag = dot3(pick2(f(ic_ref[:, 7:8] == slot), slots_ref[0]), ui_ref[0])
    next1 = new1_ref[...] - dot3(diag, u0)
    u1 = dot3(li_ref[1], next1)
    new0_c1 = pick2(f(ic_ref[:, 6:7] == slot), slots_ref[1])
    fill = dot3(dot3(li_ref[0], new0_c1), ui_ref[1])
    low0_back = dot3(rows_ref[0], ui_ref[0])
    low1_back = dot3(rows_ref[1], ui_ref[1]) - dot3(low0_back, fill)
    back = back_ref[...] - dot3(low0_back, u0) - dot3(low1_back, u1)
    copies = []
    for r in (2, 1, 0):
        rows = pl.ds(NB * r, NB)
        put = put_ref[rows, :]
        moved = sum_cols(put) > 0
        low0 = low0_ref[rows, :]
        low1 = end1_ref[rows, :] - dot3(low0, fill)
        done_ref[rows, :] = jnp.where(moved, pick2(put, back), base_ref[rows, :] - dot3(low1, u1))

        @pl.when(col == 0)
        def _():
            done_ref[rows, 0:NB] = jnp.where(moved, pick2(put, low0_back), low0)

        @pl.when(col == 1)
        def _():
            done_ref[rows, 0:NB] = jnp.where(moved, pick2(put, low1_back), low1)

        if r == 0:

            @pl.when(me == 0)
            def _():
                done_ref[0:NB, :] = u0

                @pl.when(col == 0)
                def _():
                    done_ref[0:NB, 0:NB] = new0_ref[...]

            @pl.when(me == 1)
            def _():
                done_ref[0:NB, :] = u1

                @pl.when(col == 0)
                def _():
                    done_ref[0:NB, 0:NB] = diag

                @pl.when(col == 1)
                def _():
                    done_ref[0:NB, 0:NB] = next1[:, 0:NB]

        copies.append(pltpu.make_async_copy(done_ref.at[rows, :], out_ref.at[rows, :], sem.at[r]))
        copies[-1].start()
    for copy in copies:
        copy.wait()


SCALAR = pl.BlockSpec(memory_space=pltpu.SMEM)


def call(kernel, outs, ids, *args, scratch=(), flops=0, far=(), far_out=False):
    vmem, anywhere = pl.BlockSpec(memory_space=pltpu.VMEM), pl.BlockSpec(memory_space=pl.ANY)
    smem = [] if ids is None else [SCALAR]
    sizes = [4 * o.size for o in jax.tree.leaves((outs, args))]
    return pl.pallas_call(
        kernel,
        out_shape=outs,
        in_specs=smem + [anywhere if n in far else vmem for n in range(len(args))],
        out_specs=jax.tree.map(lambda o: SCALAR if o.shape == (1,) else anywhere if far_out else vmem, outs),
        scratch_shapes=scratch,
        compiler_params=pltpu.CompilerParams(vmem_limit_bytes=40 * 1024 * 1024),
        cost_estimate=pl.CostEstimate(flops=flops, bytes_accessed=min(sizes), transcendentals=0),
    )(*([] if ids is None else [ids]), *args)


def shape(*dims, dtype=F32):
    return jax.ShapeDtypeStruct(dims, dtype)


AROUND = (4, 3, 5, 2, 6, 1, 7)


def along_x(blocks):
    return [blocks[0]] + [
        lax.ppermute(blocks[s], "x", [(i, (i + s) % 4) for i in range(4)]) for s in range(1, 4)
    ]


def fast(matrix, pivots, lower_inv, upper_inv):
    prow_idx = lax.axis_index(PROW).astype(jnp.int32)
    pcol_idx = lax.axis_index(PCOL).astype(jnp.int32)
    y_idx, core_idx = lax.axis_index("y"), lax.axis_index("core")
    ids = jnp.stack([prow_idx, pcol_idx, y_idx, core_idx]).astype(jnp.int32)
    part = RD // 8
    rows, ir, ic, most, *panel = call(
        pack_kernel,
        (
            shape(NP, 5, 2, RD), shape(8, NB, dtype=jnp.int32), shape(NB, 8, dtype=jnp.int32),
            shape(1, dtype=jnp.int32), *[shape(part, NB)] * 8,
        ),
        ids, pivots, matrix, flops=10**6,
    )
    rows_in = lax.all_to_all(rows, PROW, 0, 0)
    piece = jnp.where(y_idx == 0, panel[0], F32(0.0))
    for k in AROUND:
        piece = piece + lax.ppermute(panel[k], "y", [(0, k)])
    rows_in, piece = lax.optimization_barrier((rows_in, piece))
    raw = lax.all_gather(piece, PCOL, tiled=True).reshape(8, 2, part, NB)
    send, side = call(
        turn_kernel, (shape(8, 24, RD), shape(80, NB)), ids, ir, ic, rows_in,
        scratch=[pltpu.VMEM((16, RD), F32), pltpu.VMEM((2 * NP, RD), F32)], flops=10**6,
    )
    main_z = lax.all_to_all(send, "z", 0, 0)
    parts = [lax.ppermute(side, "y", [(0, k)]) for k in AROUND]
    side_send = call(
        side_kernel, [shape(64, 128)] * 4, ids, side, *parts, scratch=[pltpu.VMEM((80, NB), F32)]
    )
    side_x = along_x(side_send)
    main_x = along_x(call(mid_kernel, [shape(144, RD)] * 4, ids, main_z))
    mine = lax.all_to_all(call(join_kernel, shape(8, 144, 128), None, *side_x), "z", 0, 0)
    mine, main_x, raw = lax.optimization_barrier((mine, main_x, raw))
    there = lax.ppermute(mine, "core", [(0, 1), (1, 0)])
    base, put, back, new0, new1, u0, low0, end1 = call(
        main_kernel,
        (
            shape(RD, RD), shape(RD, 2 * NP), shape(2 * NP, RD), shape(NB, NB), shape(NB, RD),
            shape(NB, RD), shape(RD, NB), shape(RD, NB),
        ),
        ids, ir, ic, matrix, *main_x, lower_inv, upper_inv, raw, far=(9,),
        scratch=[pltpu.VMEM((8, 2, part, NB), F32), pltpu.SemaphoreType.DMA],
    )
    out = call(
        final_kernel, shape(RD, RD), ids, ic, mine, there, base, put, back, new0, new1, u0,
        low0, end1, lower_inv, upper_inv, far_out=True,
        scratch=[
            pltpu.VMEM((RD, RD), F32), pltpu.VMEM((2, 2 * NB, NB), F32),
            pltpu.VMEM((2, 2 * NP, NB), F32), pltpu.SemaphoreType.DMA((3,)),
        ],
    )
    return out, most[0]


def broadcast(value, axis, root):
    mine = lax.axis_index(axis) == root
    return lax.psum(jnp.where(mine, value, jnp.zeros_like(value)), axis)


def general(matrix, pivots, lower_inv, upper_inv):
    current = matrix
    rows_dev = current.shape[0]
    cols_dev = current.shape[1]
    panel_width = pivots.shape[1]
    prow_idx = lax.axis_index(PROW)
    pcol_idx = lax.axis_index(PCOL)
    row_pos = jnp.arange(rows_dev)
    col_pos = jnp.arange(cols_dev)
    row_done = jnp.zeros((rows_dev,), bool)
    col_done = jnp.zeros((cols_dev,), bool)
    for panel_no in range(2):
        row_done = row_done | (prow_idx == panel_no) & (row_pos < panel_width)
        col_done = col_done | (pcol_idx == panel_no) & (col_pos < panel_width)
        pivot_list = pivots[panel_no]
        owner_row = pivot_list // rows_dev
        local_row = pivot_list % rows_dev
        is_owned = owner_row == prow_idx
        on_root = prow_idx == panel_no
        old_block = broadcast(current[:panel_width], PROW, panel_no)
        pivot_data = jnp.where(is_owned[:, None], current[local_row], F32(0.0))
        new_rows = lax.psum(pivot_data, PROW)
        upper_rows = hdot(lower_inv[panel_no], new_rows)
        row_block = jnp.where(col_done[None, :], new_rows, upper_rows)
        target = jnp.where(is_owned, local_row, rows_dev)
        current = current.at[target].set(old_block, mode="drop")
        current = current.at[:panel_width].set(jnp.where(on_root, row_block, current[:panel_width]))
        lower_here = hdot(current[:, :panel_width], upper_inv[panel_no])
        lower_cols = broadcast(lower_here, PCOL, panel_no)
        rank_update = hdot(lower_cols, row_block)
        keep_mask = (~row_done)[:, None] & (~col_done)[None, :]
        current = jnp.where(keep_mask, current - rank_update, current)
        panel_mask = (pcol_idx == panel_no) & (~row_done)[:, None]
        current = current.at[:, :panel_width].set(
            jnp.where(panel_mask, lower_cols, current[:, :panel_width])
        )
    return current


def local(matrix, pivots, lower_inv, upper_inv):
    def body(state):
        out = general(with_layout_constraint(matrix, ROW_MAJOR), pivots, lower_inv, upper_inv)
        return jnp.zeros((), bool), with_layout_constraint(out, ROW_MAJOR)

    quick, most = fast(matrix, pivots, lower_inv, upper_inv)
    return lax.while_loop(lambda state: state[0], body, (most > NP, quick))[1]


def solution(mesh):
    grid = Mesh(mesh.devices.reshape(8, 4, 8, 2), ("z", "x", "y", "core"))
    in_specs = (P(PROW, PCOL), P(), P(), P())
    return jax.shard_map(local, mesh=grid, in_specs=in_specs, out_specs=P(PROW, PCOL), check_vma=False)
```

```python
import functools

import jax
import jax.numpy as jnp
from jax import lax
from jax.experimental import pallas as pl
from jax.experimental.layout import Layout, with_layout_constraint
from jax.experimental.pallas import tpu as pltpu
from jax.sharding import Mesh, PartitionSpec as P

HIGHEST = lax.Precision.HIGHEST
F32 = jnp.float32
BF16 = jnp.bfloat16
NB = 256
RD = 768
PROW = ("z", "x")
PCOL = ("y", "core")
NP = 32
ROW_MAJOR = Layout((0, 1))


def hdot(a, b):
    return jnp.dot(a, b, precision=HIGHEST, preferred_element_type=F32)


def iota(shape, dim):
    return lax.broadcasted_iota(jnp.int32, shape, dim)


def f(mask):
    return jnp.where(mask, F32(1.0), F32(0.0))


def sum_rows(x):
    return jnp.sum(x, axis=0, keepdims=True)


def sum_cols(x):
    return jnp.sum(x, axis=1, keepdims=True)


def owner_of(row):
    return ((row >> 8) * 171) >> 9


def slot_of(rank, g):
    return ((rank & 3) * 128 + ((rank >> 2) & 7) * 16 + g * 8 + (rank >> 5)).astype(F32)


def index_math(pr, pc):
    p0r, p1r = pr[0:1, :], pr[1:2, :]
    p0c, p1c = pc
    sub, lane = iota((NB, NB), 0), iota((NB, NB), 1)
    lr, lc = iota((1, NB), 1), iota((NB, 1), 0)
    m_kj = f(p0c == lane + RD)
    n_kj = f(p0c == p1r)
    m_jk = f(p0r == sub + RD)
    n_jk = f(p0r == p1c)
    p1rf, p1cf = p1r.astype(F32), p1c.astype(F32)

    def dest(p0, p1, ids, has_m, has_n, piv_m, has_mk):
        stay0 = (p0 == ids) | (has_n > 0)
        end0 = jnp.where(has_m > 0, piv_m.astype(jnp.int32), p0)
        stay1 = (p1 == ids + RD) | (has_mk > 0)
        out = []
        for stay, end in ((stay0, end0), (stay1, p1)):
            own = owner_of(end)
            out.append((jnp.where(stay, NP, own), end - own * RD))
        return out

    has_m_c, has_n_c = sum_cols(m_kj), sum_cols(n_kj)
    has_m_r, has_n_r = sum_rows(m_jk), sum_rows(n_jk)
    has_mk_r, has_nk_r = sum_rows(m_kj), sum_rows(n_kj)
    has_mk_c, has_nk_c = sum_cols(m_jk), sum_cols(n_jk)
    dest_r = dest(p0r, p1r, lr, has_m_r, has_n_r, sum_rows(m_jk * p1cf), has_mk_r)
    dest_c = dest(p0c, p1c, lc, has_m_c, has_n_c, sum_cols(m_kj * p1rf), has_mk_c)
    ranks_r, ranks_c, pos_r, pos_c = [], [], [], []
    for g in range(2):
        key_r = dest_r[g][0] * NB + lr
        key_c = dest_c[g][0] * NB + lc
        rank_r = sum_rows(f(key_c < key_r)).astype(jnp.int32)
        rank_c = sum_cols(f(key_r < key_c)).astype(jnp.int32)
        ranks_r.append(rank_r)
        ranks_c.append(rank_c)
        pos_r.append(slot_of(rank_r, g))
        pos_c.append(slot_of(rank_c, g))
    w_r = jnp.where(has_mk_r > 0, sum_rows(m_kj * pos_c[0]), pos_r[1])
    w_c = jnp.where(has_mk_c > 0, sum_cols(m_jk * pos_r[0]), pos_c[1])
    src0 = jnp.where(
        has_m_c > 0,
        sum_cols(m_kj * pos_r[1]),
        jnp.where(has_n_c > 0, sum_cols(n_kj * w_r), pos_c[0]),
    )
    src1 = jnp.where(has_nk_c > 0, sum_cols(n_jk * pos_r[0]), w_c)
    rows, cols = [], []
    for g in range(2):
        rows += [ranks_r[g], dest_r[g][0], dest_r[g][1]]
        cols += [ranks_c[g], dest_c[g][0], dest_c[g][1]]
    cols += [src0.astype(jnp.int32), src1.astype(jnp.int32)]
    return rows, cols


def bdot(a, b):
    return jnp.dot(a, b, preferred_element_type=F32)


def halves(x):
    hi = x.astype(BF16)
    return hi, (x - hi.astype(F32)).astype(BF16)


def dot3(a, b):
    ah, al = halves(a)
    bh, bl = halves(b)
    return bdot(jnp.concatenate([ah, ah, al], axis=1), jnp.concatenate([bh, bl, bh], axis=0))


def pick2(p, x):
    p = p.astype(BF16)
    hi, lo = halves(x)
    return bdot(jnp.concatenate([p, p], axis=1), jnp.concatenate([hi, lo], axis=0))


def pick3(p, x):
    p = p.astype(BF16)
    hi = x.astype(BF16)
    rest = x - hi.astype(F32)
    mid = rest.astype(BF16)
    low = (rest - mid.astype(F32)).astype(BF16)
    return bdot(p, hi) + (bdot(p, mid) + bdot(p, low))


def pack_kernel(ids, p_ref, a_ref, send_ref, ir_ref, ic_ref, most_ref, *piece_refs):
    me = ids[0]
    for n, r in enumerate(piece_refs):
        rows_n = r.shape[0]
        r[...] = a_ref[rows_n * n : rows_n * (n + 1), 0:NB]
    pr = p_ref[...]
    eye = iota((NB, NB), 0) == iota((NB, NB), 1)
    turned = [sum_cols(jnp.where(eye, pr[n : n + 1, :].astype(F32), F32(0.0))) for n in range(2)]
    rows, cols = index_math(pr, [t.astype(jnp.int32) for t in turned])
    for n, v in enumerate(rows):
        ir_ref[n : n + 1, :] = v
    ir_ref[6:8, :] = jnp.zeros((2, NB), jnp.int32)
    for n, v in enumerate(cols):
        ic_ref[:, n : n + 1] = v
    counts = [sum_rows(f(cols[3 * g + 1] == iota((NB, NP), 1))) for g in range(2)]
    most_ref[0] = jnp.max(jnp.maximum(counts[0], counts[1])).astype(jnp.int32)
    line = iota((NB, NB), 0)
    rank = jnp.where(me == 1, rows[3], rows[0])
    perm = f(rank == (line >> 3) + NP * (line & 7))
    old = pick3(perm, a_ref[0:NB, :])
    line = iota((2 * NP, NB), 0)
    pick = jnp.zeros((2 * NP, RD), F32)
    for g in range(2):
        rank, own = rows[3 * g], rows[3 * g + 1]
        s = f(((line & 1) == g) & ((rank & 31) == (line >> 1)) & (own == me))
        t = f(cols[3 * g + 2] == iota((NB, RD), 1))
        pick = pick + bdot(s.astype(BF16), t.astype(BF16))
    ext = pick3(pick, a_ref[...])
    for m in range(NP):
        for q in range(4):
            send_ref[m, q] = old[8 * m + 2 * q : 8 * m + 2 * q + 2]
        send_ref[m, 4] = ext[2 * m : 2 * m + 2]


def turn_kernel(ids, ir_ref, ic_ref, in_ref, send_ref, old_ref, ext_ref):
    me = ids[0]
    for q in range(4):
        old_ref[2 * q : 2 * q + 2, :] = in_ref[0, q]
        old_ref[8 + 2 * q : 10 + 2 * q, :] = in_ref[1, q]
    for m in range(NP):
        ext_ref[2 * m : 2 * m + 2, :] = in_ref[m, 4]
    line = iota((16, NB), 0)
    want = me + NP * (line & 7)
    own = jnp.zeros((16, 1), F32)
    for g in range(2):
        hit = f((ir_ref[3 * g : 3 * g + 1, :] == want) & ((line >> 3) == g))
        own = own + sum_cols(hit * ir_ref[3 * g + 1 : 3 * g + 2, :].astype(F32))
    own = own.astype(jnp.int32)
    old = old_ref[...]
    lane = iota((16, 2 * NP), 1)
    pick = f((own == (lane >> 1)) & ((iota((16, 2 * NP), 0) >> 3) == (lane & 1)))
    slots = jnp.where(own == NP, old, pick3(pick, ext_ref[...]))
    want = me + NP * (iota((NB, 16), 1) & 7)
    own = jnp.zeros((1, 16), F32)
    for g in range(2):
        hit = f((ic_ref[:, 3 * g : 3 * g + 1] == want) & ((iota((NB, 16), 1) >> 3) == g))
        own = own + sum_rows(hit * ic_ref[:, 3 * g + 1 : 3 * g + 2].astype(F32))
    own = own.astype(jnp.int32)
    line = iota((2 * NP, 16), 0)
    give = f((own == (line >> 1)) & ((iota((2 * NP, 16), 1) >> 3) == (line & 1)))
    back = pick3(give, old)
    for z in range(8):
        send_ref[z, 0:16, :] = slots
        send_ref[z, 16:24, :] = back[8 * z : 8 * z + 8]


def arrange(get, out_ref):
    for x in range(4):
        for z in range(8):
            out_ref[x, 16 * z : 16 * z + 16, :] = get(z, 0, 16)
            out_ref[x, 128 + 2 * z : 130 + 2 * z, :] = get(z, 16 + 2 * x, 18 + 2 * x)


def mid_kernel(in_ref, out_ref, side_ref):
    arrange(lambda z, a, b: in_ref[z, a:b, :], out_ref)
    for z in range(8):
        side_ref[24 * z : 24 * z + 24, :] = in_ref[z, :, 0:NB]


def side_kernel(ids, *refs):
    own, out, sums = refs[0], refs[8], refs[9]
    total = jnp.where(ids[2] == 0, own[...], F32(0.0))
    for r in refs[1:8]:
        total = total + r[...]
    sums[...] = total
    arrange(lambda z, a, b: sums[24 * z + a : 24 * z + b, :], out)


KEPT = {
    "base": (RD, RD), "new1": (NB, RD), "u0": (NB, RD), "low0": (RD, NB), "end1": (RD, NB),
    "put": (RD, 2 * NP), "back": (2 * NP, RD), "new0": (NB, NB),
}


def main_kernel(ids, ir_ref, ic_ref, a_ref, x_ref, li_ref, ui_ref, raw_ref, *refs):
    me = ids[0]
    count = len(KEPT)
    held_ref, here_ref, fetch_sem, store_sem = refs[2 * count :]
    far = dict(zip(KEPT, refs[:count]))
    near = dict(zip(KEPT, refs[count : 2 * count]))
    fetches = [
        pltpu.make_async_copy(raw_ref, held_ref, fetch_sem.at[0]),
        pltpu.make_async_copy(a_ref, here_ref, fetch_sem.at[1]),
    ]
    for fetch in fetches:
        fetch.start()
    stores = []

    def keep(name, value=None):
        if value is not None:
            near[name][...] = value
        stores.append(pltpu.make_async_copy(near[name], far[name], store_sem.at[len(stores)]))
        stores[-1].start()

    put = jnp.zeros((RD, 2 * NP), F32)
    lane = iota((NB, 2 * NP), 1)
    m = ((lane >> 1) & 7) * 4 + (lane >> 4)
    for g in range(2):
        own, loc = ir_ref[3 * g + 1 : 3 * g + 2, :], ir_ref[3 * g + 2 : 3 * g + 3, :]
        t = f((own == me) & (loc == iota((RD, NB), 0)))
        s = f(((ic_ref[:, 3 * g : 3 * g + 1] & 31) == m) & ((lane & 1) == g))
        put = put + bdot(t.astype(BF16), s.astype(BF16))
    keep("put", put)
    keep("back", jnp.concatenate([x_ref[x, 128:144, :] for x in range(4)], axis=0))
    slots = jnp.concatenate([x_ref[x, 0:128, :] for x in range(4)], axis=0)
    slot = iota((NB, 2 * NB), 1)
    new0 = pick2(f(ic_ref[:, 6:7] == slot), slots)
    keep("new0", new0[:, 0:NB])
    keep("new1", pick2(f(ic_ref[:, 7:8] == slot), slots))
    u0 = dot3(li_ref[0], new0)
    keep("u0", u0)
    fetches[0].wait()
    for n, name in enumerate(("low0", "end1")):
        raw = jnp.concatenate([held_ref[y, n] for y in range(8)], axis=0)
        keep(name, dot3(raw, ui_ref[n]))
    fetches[1].wait()
    for r in range(3):
        rows = pl.ds(NB * r, NB)
        near["base"][rows, :] = here_ref[rows, :] - dot3(near["low0"][rows, :], u0)
    keep("base")
    for store in stores:
        store.wait()


def final_kernel(ids, ic_ref, mine_ref, there_ref, li_ref, ui_ref, *refs):
    me, col, core = ids[0], ids[1], ids[3]
    count = len(KEPT)
    out_ref, done_ref, sem, fetch_sem = refs[count], *refs[2 * count + 1 :]
    near = dict(zip(KEPT, refs[count + 1 : 2 * count + 1]))
    fetches = {}
    order = ("u0", "new1", "back", "low0", "end1", "put", "base", "new0")
    for n, name in enumerate(order):
        far = refs[list(KEPT).index(name)]
        fetches[name] = pltpu.make_async_copy(far, near[name], fetch_sem.at[n])
        fetches[name].start()
    mine, there = mine_ref[...], there_ref[...]
    sides = [jnp.where(core == k, mine, there) for k in range(2)]
    slots = [jnp.concatenate([v[x, 0:128] for x in range(4)], axis=0) for v in sides]
    rows_back = [jnp.concatenate([v[x, 128:144] for x in range(4)], axis=0) for v in sides]
    slot = iota((NB, 2 * NB), 1)
    diag = dot3(pick2(f(ic_ref[:, 7:8] == slot), slots[0]), ui_ref[0])
    new0_c1 = pick2(f(ic_ref[:, 6:7] == slot), slots[1])
    fill = dot3(dot3(li_ref[0], new0_c1), ui_ref[1])
    low0_back = dot3(rows_back[0], ui_ref[0])
    low1_back = dot3(rows_back[1], ui_ref[1]) - dot3(low0_back, fill)
    for name in order[:3]:
        fetches[name].wait()
    u0 = near["u0"][...]
    next1 = near["new1"][...] - dot3(diag, u0)
    u1 = dot3(li_ref[1], next1)
    back = near["back"][...] - dot3(low0_back, u0) - dot3(low1_back, u1)
    for name in order[3:]:
        fetches[name].wait()
    copies = []
    for r in (2, 1, 0):
        rows = pl.ds(NB * r, NB)
        put = near["put"][rows, :]
        moved = sum_cols(put) > 0
        low0 = near["low0"][rows, :]
        low1 = near["end1"][rows, :] - dot3(low0, fill)
        done_ref[rows, :] = jnp.where(moved, pick2(put, back), near["base"][rows, :] - dot3(low1, u1))

        @pl.when(col == 0)
        def _():
            done_ref[rows, 0:NB] = jnp.where(moved, pick2(put, low0_back), low0)

        @pl.when(col == 1)
        def _():
            done_ref[rows, 0:NB] = jnp.where(moved, pick2(put, low1_back), low1)

        if r == 0:

            @pl.when(me == 0)
            def _():
                done_ref[0:NB, :] = u0

                @pl.when(col == 0)
                def _():
                    done_ref[0:NB, 0:NB] = near["new0"][...]

            @pl.when(me == 1)
            def _():
                done_ref[0:NB, :] = u1

                @pl.when(col == 0)
                def _():
                    done_ref[0:NB, 0:NB] = diag

                @pl.when(col == 1)
                def _():
                    done_ref[0:NB, 0:NB] = next1[:, 0:NB]

        copies.append(pltpu.make_async_copy(done_ref.at[rows, :], out_ref.at[rows, :], sem.at[r]))
        copies[-1].start()
    for copy in copies:
        copy.wait()


SCALAR = pl.BlockSpec(memory_space=pltpu.SMEM)


def call(kernel, outs, ids, *args, scratch=(), flops=0, far=(), far_out=False):
    vmem, anywhere = pl.BlockSpec(memory_space=pltpu.VMEM), pl.BlockSpec(memory_space=pl.ANY)
    smem = [] if ids is None else [SCALAR]
    sizes = [4 * o.size for o in jax.tree.leaves((outs, args))]
    return pl.pallas_call(
        kernel,
        out_shape=outs,
        in_specs=smem + [anywhere if n in far else vmem for n in range(len(args))],
        out_specs=jax.tree.map(lambda o: SCALAR if o.shape == (1,) else anywhere if far_out else vmem, outs),
        scratch_shapes=scratch,
        compiler_params=pltpu.CompilerParams(vmem_limit_bytes=(60 if far_out else 40) * 1024 * 1024),
        cost_estimate=pl.CostEstimate(flops=flops, bytes_accessed=min(sizes), transcendentals=0),
    )(*([] if ids is None else [ids]), *args)


def shape(*dims, dtype=F32):
    return jax.ShapeDtypeStruct(dims, dtype)


AROUND = (4, 3, 5, 2, 6, 1, 7)


def fast(matrix, pivots, lower_inv, upper_inv):
    prow_idx = lax.axis_index(PROW).astype(jnp.int32)
    pcol_idx = lax.axis_index(PCOL).astype(jnp.int32)
    y_idx, core_idx = lax.axis_index("y"), lax.axis_index("core")
    ids = jnp.stack([prow_idx, pcol_idx, y_idx, core_idx]).astype(jnp.int32)
    part = RD // 8
    rows, ir, ic, most, *panel = call(
        pack_kernel,
        (
            shape(NP, 5, 2, RD), shape(8, NB, dtype=jnp.int32), shape(NB, 8, dtype=jnp.int32),
            shape(1, dtype=jnp.int32), *[shape(part, NB)] * 8,
        ),
        ids, pivots, matrix, flops=10**6,
    )
    rows_in = lax.all_to_all(rows, PROW, 0, 0)
    piece = jnp.where(y_idx == 0, panel[0], F32(0.0))
    for k in AROUND:
        piece = piece + lax.ppermute(panel[k], "y", [(0, k)])
    rows_in, piece = lax.optimization_barrier((rows_in, piece))
    raw = lax.all_gather(piece, PCOL, tiled=True).reshape(8, 2, part, NB)
    send = call(
        turn_kernel, shape(8, 24, RD), ids, ir, ic, rows_in,
        scratch=[pltpu.VMEM((16, RD), F32), pltpu.VMEM((2 * NP, RD), F32)],
    )
    main_z = lax.all_to_all(send, "z", 0, 0)
    main_send, side = call(mid_kernel, (shape(4, 144, RD), shape(192, NB)), None, main_z)
    main_x = lax.all_to_all(main_send, "x", 0, 0)
    parts = [lax.ppermute(side, "y", [(0, k)]) for k in AROUND]
    side_send = call(
        side_kernel, shape(4, 144, NB), ids, side, *parts, scratch=[pltpu.VMEM((192, NB), F32)]
    )
    side_send, main_x, raw = lax.optimization_barrier((side_send, main_x, raw))
    mine = lax.all_to_all(side_send, "x", 0, 0)
    near = [pltpu.VMEM(dims, F32) for dims in KEPT.values()]
    kept = call(
        main_kernel, [shape(*dims) for dims in KEPT.values()],
        ids, ir, ic, matrix, main_x, lower_inv, upper_inv, raw, far=(2, 6), far_out=True,
        scratch=near + [
            pltpu.VMEM((8, 2, part, NB), F32), pltpu.VMEM((RD, RD), F32),
            pltpu.SemaphoreType.DMA((2,)), pltpu.SemaphoreType.DMA((len(KEPT),)),
        ],
    )
    mine, kept = lax.optimization_barrier((mine, kept))
    there = lax.ppermute(mine, "core", [(0, 1), (1, 0)])
    out = call(
        final_kernel, shape(RD, RD), ids, ic, mine, there, lower_inv, upper_inv, *kept,
        far=tuple(range(5, 5 + len(KEPT))), far_out=True,
        scratch=near + [
            pltpu.VMEM((RD, RD), F32), pltpu.SemaphoreType.DMA((3,)),
            pltpu.SemaphoreType.DMA((len(KEPT),)),
        ],
    )
    return out, most[0]


def broadcast(value, axis, root):
    mine = lax.axis_index(axis) == root
    return lax.psum(jnp.where(mine, value, jnp.zeros_like(value)), axis)


def general(matrix, pivots, lower_inv, upper_inv):
    current = matrix
    rows_dev = current.shape[0]
    cols_dev = current.shape[1]
    panel_width = pivots.shape[1]
    prow_idx = lax.axis_index(PROW)
    pcol_idx = lax.axis_index(PCOL)
    row_pos = jnp.arange(rows_dev)
    col_pos = jnp.arange(cols_dev)
    row_done = jnp.zeros((rows_dev,), bool)
    col_done = jnp.zeros((cols_dev,), bool)
    for panel_no in range(2):
        row_done = row_done | (prow_idx == panel_no) & (row_pos < panel_width)
        col_done = col_done | (pcol_idx == panel_no) & (col_pos < panel_width)
        pivot_list = pivots[panel_no]
        owner_row = pivot_list // rows_dev
        local_row = pivot_list % rows_dev
        is_owned = owner_row == prow_idx
        on_root = prow_idx == panel_no
        old_block = broadcast(current[:panel_width], PROW, panel_no)
        pivot_data = jnp.where(is_owned[:, None], current[local_row], F32(0.0))
        new_rows = lax.psum(pivot_data, PROW)
        upper_rows = hdot(lower_inv[panel_no], new_rows)
        row_block = jnp.where(col_done[None, :], new_rows, upper_rows)
        target = jnp.where(is_owned, local_row, rows_dev)
        current = current.at[target].set(old_block, mode="drop")
        current = current.at[:panel_width].set(jnp.where(on_root, row_block, current[:panel_width]))
        lower_here = hdot(current[:, :panel_width], upper_inv[panel_no])
        lower_cols = broadcast(lower_here, PCOL, panel_no)
        rank_update = hdot(lower_cols, row_block)
        keep_mask = (~row_done)[:, None] & (~col_done)[None, :]
        current = jnp.where(keep_mask, current - rank_update, current)
        panel_mask = (pcol_idx == panel_no) & (~row_done)[:, None]
        current = current.at[:, :panel_width].set(
            jnp.where(panel_mask, lower_cols, current[:, :panel_width])
        )
    return current


def local(matrix, pivots, lower_inv, upper_inv):
    def body(state):
        out = general(with_layout_constraint(matrix, ROW_MAJOR), pivots, lower_inv, upper_inv)
        return jnp.zeros((), bool), with_layout_constraint(out, ROW_MAJOR)

    quick, most = fast(matrix, pivots, lower_inv, upper_inv)
    return lax.while_loop(lambda state: state[0], body, (most > NP, quick))[1]


def solution(mesh):
    grid = Mesh(mesh.devices.reshape(8, 4, 8, 2), ("z", "x", "y", "core"))
    in_specs = (P(PROW, PCOL), P(), P(), P())
    return jax.shard_map(local, mesh=grid, in_specs=in_specs, out_specs=P(PROW, PCOL), check_vma=False)
```

```python
import functools

import jax
import jax.numpy as jnp
from jax import lax
from jax.experimental import pallas as pl
from jax.experimental.layout import Layout, with_layout_constraint
from jax.experimental.pallas import tpu as pltpu
from jax.sharding import Mesh, PartitionSpec as P

HIGHEST = lax.Precision.HIGHEST
F32 = jnp.float32
BF16 = jnp.bfloat16
NB = 256
RD = 768
PROW = ("z", "x")
PCOL = ("y", "core")
NP = 32
ROW_MAJOR = Layout((0, 1))


def hdot(a, b):
    return jnp.dot(a, b, precision=HIGHEST, preferred_element_type=F32)


def iota(shape, dim):
    return lax.broadcasted_iota(jnp.int32, shape, dim)


def f(mask):
    return jnp.where(mask, F32(1.0), F32(0.0))


def sum_rows(x):
    return jnp.sum(x, axis=0, keepdims=True)


def sum_cols(x):
    return jnp.sum(x, axis=1, keepdims=True)


def owner_of(row):
    return ((row >> 8) * 171) >> 9


def slot_of(rank, g):
    return ((rank & 3) * 128 + ((rank >> 2) & 7) * 16 + g * 8 + (rank >> 5)).astype(F32)


def index_math(pr, pc):
    p0r, p1r = pr[0:1, :], pr[1:2, :]
    p0c, p1c = pc
    sub, lane = iota((NB, NB), 0), iota((NB, NB), 1)
    lr, lc = iota((1, NB), 1), iota((NB, 1), 0)
    m_kj = f(p0c == lane + RD)
    n_kj = f(p0c == p1r)
    m_jk = f(p0r == sub + RD)
    n_jk = f(p0r == p1c)
    p1rf, p1cf = p1r.astype(F32), p1c.astype(F32)

    def dest(p0, p1, ids, has_m, has_n, piv_m, has_mk):
        stay0 = (p0 == ids) | (has_n > 0)
        end0 = jnp.where(has_m > 0, piv_m.astype(jnp.int32), p0)
        stay1 = (p1 == ids + RD) | (has_mk > 0)
        out = []
        for stay, end in ((stay0, end0), (stay1, p1)):
            own = owner_of(end)
            out.append((jnp.where(stay, NP, own), end - own * RD))
        return out

    has_m_c, has_n_c = sum_cols(m_kj), sum_cols(n_kj)
    has_m_r, has_n_r = sum_rows(m_jk), sum_rows(n_jk)
    has_mk_r, has_nk_r = sum_rows(m_kj), sum_rows(n_kj)
    has_mk_c, has_nk_c = sum_cols(m_jk), sum_cols(n_jk)
    dest_r = dest(p0r, p1r, lr, has_m_r, has_n_r, sum_rows(m_jk * p1cf), has_mk_r)
    dest_c = dest(p0c, p1c, lc, has_m_c, has_n_c, sum_cols(m_kj * p1rf), has_mk_c)
    ranks_r, ranks_c, pos_r, pos_c = [], [], [], []
    for g in range(2):
        key_r = dest_r[g][0] * NB + lr
        key_c = dest_c[g][0] * NB + lc
        rank_r = sum_rows(f(key_c < key_r)).astype(jnp.int32)
        rank_c = sum_cols(f(key_r < key_c)).astype(jnp.int32)
        ranks_r.append(rank_r)
        ranks_c.append(rank_c)
        pos_r.append(slot_of(rank_r, g))
        pos_c.append(slot_of(rank_c, g))
    w_r = jnp.where(has_mk_r > 0, sum_rows(m_kj * pos_c[0]), pos_r[1])
    w_c = jnp.where(has_mk_c > 0, sum_cols(m_jk * pos_r[0]), pos_c[1])
    src0 = jnp.where(
        has_m_c > 0,
        sum_cols(m_kj * pos_r[1]),
        jnp.where(has_n_c > 0, sum_cols(n_kj * w_r), pos_c[0]),
    )
    src1 = jnp.where(has_nk_c > 0, sum_cols(n_jk * pos_r[0]), w_c)
    rows, cols = [], []
    for g in range(2):
        rows += [ranks_r[g], dest_r[g][0], dest_r[g][1]]
        cols += [ranks_c[g], dest_c[g][0], dest_c[g][1]]
    cols += [src0.astype(jnp.int32), src1.astype(jnp.int32)]
    return rows, cols


def bdot(a, b):
    return jnp.dot(a, b, preferred_element_type=F32)


def halves(x):
    hi = x.astype(BF16)
    return hi, (x - hi.astype(F32)).astype(BF16)


def dot3(a, b):
    ah, al = halves(a)
    bh, bl = halves(b)
    return bdot(jnp.concatenate([ah, ah, al], axis=1), jnp.concatenate([bh, bl, bh], axis=0))


def pick2(p, x):
    p = p.astype(BF16)
    hi, lo = halves(x)
    return bdot(jnp.concatenate([p, p], axis=1), jnp.concatenate([hi, lo], axis=0))


def pick3(p, x):
    p = p.astype(BF16)
    hi = x.astype(BF16)
    rest = x - hi.astype(F32)
    mid = rest.astype(BF16)
    low = (rest - mid.astype(F32)).astype(BF16)
    return bdot(p, hi) + (bdot(p, mid) + bdot(p, low))


def pack_kernel(ids, p_ref, a_ref, send_ref, ir_ref, ic_ref, most_ref, *piece_refs):
    me = ids[0]
    for n, r in enumerate(piece_refs):
        rows_n = r.shape[0]
        r[...] = a_ref[rows_n * n : rows_n * (n + 1), 0:NB]
    pr = p_ref[...]
    eye = iota((NB, NB), 0) == iota((NB, NB), 1)
    turned = [sum_cols(jnp.where(eye, pr[n : n + 1, :].astype(F32), F32(0.0))) for n in range(2)]
    rows, cols = index_math(pr, [t.astype(jnp.int32) for t in turned])
    for n, v in enumerate(rows):
        ir_ref[n : n + 1, :] = v
    ir_ref[6:8, :] = jnp.zeros((2, NB), jnp.int32)
    for n, v in enumerate(cols):
        ic_ref[:, n : n + 1] = v
    counts = [sum_rows(f(cols[3 * g + 1] == iota((NB, NP), 1))) for g in range(2)]
    most_ref[0] = jnp.max(jnp.maximum(counts[0], counts[1])).astype(jnp.int32)
    line = iota((NB, NB), 0)
    rank = jnp.where(me == 1, rows[3], rows[0])
    perm = f(rank == (line >> 3) + NP * (line & 7))
    old = pick3(perm, a_ref[0:NB, :])
    line = iota((2 * NP, NB), 0)
    pick = jnp.zeros((2 * NP, RD), F32)
    for g in range(2):
        rank, own = rows[3 * g], rows[3 * g + 1]
        s = f(((line & 1) == g) & ((rank & 31) == (line >> 1)) & (own == me))
        t = f(cols[3 * g + 2] == iota((NB, RD), 1))
        pick = pick + bdot(s.astype(BF16), t.astype(BF16))
    ext = pick3(pick, a_ref[...])
    for m in range(NP):
        for q in range(4):
            send_ref[m, q] = old[8 * m + 2 * q : 8 * m + 2 * q + 2]
        send_ref[m, 4] = ext[2 * m : 2 * m + 2]


def turn_kernel(ids, ir_ref, ic_ref, in_ref, send_ref, old_ref, ext_ref):
    me = ids[0]
    for q in range(4):
        old_ref[2 * q : 2 * q + 2, :] = in_ref[0, q]
        old_ref[8 + 2 * q : 10 + 2 * q, :] = in_ref[1, q]
    for m in range(NP):
        ext_ref[2 * m : 2 * m + 2, :] = in_ref[m, 4]
    line = iota((16, NB), 0)
    want = me + NP * (line & 7)
    own = jnp.zeros((16, 1), F32)
    for g in range(2):
        hit = f((ir_ref[3 * g : 3 * g + 1, :] == want) & ((line >> 3) == g))
        own = own + sum_cols(hit * ir_ref[3 * g + 1 : 3 * g + 2, :].astype(F32))
    own = own.astype(jnp.int32)
    old = old_ref[...]
    lane = iota((16, 2 * NP), 1)
    pick = f((own == (lane >> 1)) & ((iota((16, 2 * NP), 0) >> 3) == (lane & 1)))
    slots = jnp.where(own == NP, old, pick3(pick, ext_ref[...]))
    want = me + NP * (iota((NB, 16), 1) & 7)
    own = jnp.zeros((1, 16), F32)
    for g in range(2):
        hit = f((ic_ref[:, 3 * g : 3 * g + 1] == want) & ((iota((NB, 16), 1) >> 3) == g))
        own = own + sum_rows(hit * ic_ref[:, 3 * g + 1 : 3 * g + 2].astype(F32))
    own = own.astype(jnp.int32)
    line = iota((2 * NP, 16), 0)
    give = f((own == (line >> 1)) & ((iota((2 * NP, 16), 1) >> 3) == (line & 1)))
    back = pick3(give, old)
    for z in range(8):
        send_ref[z, 0:16, :] = slots
        send_ref[z, 16:24, :] = back[8 * z : 8 * z + 8]


def arrange(get, out_ref):
    for x in range(4):
        for z in range(8):
            out_ref[x, 16 * z : 16 * z + 16, :] = get(z, 0, 16)
            out_ref[x, 128 + 2 * z : 130 + 2 * z, :] = get(z, 16 + 2 * x, 18 + 2 * x)


def mid_kernel(in_ref, out_ref, side_ref):
    arrange(lambda z, a, b: in_ref[z, a:b, :], out_ref)
    for z in range(8):
        side_ref[24 * z : 24 * z + 24, :] = in_ref[z, :, 0:NB]


def side_kernel(ids, *refs):
    own, out, sums = refs[0], refs[8], refs[9]
    total = jnp.where(ids[2] == 0, own[...], F32(0.0))
    for r in refs[1:8]:
        total = total + r[...]
    sums[...] = total
    arrange(lambda z, a, b: sums[24 * z + a : 24 * z + b, :], out)


KEPT = {
    "base": (RD, RD), "lead1": (NB, RD), "u0": (NB, RD), "low0": (RD, NB), "end1": (RD, NB),
    "put": (RD, 2 * NP), "back": (2 * NP, RD), "new0": (NB, NB), "new1": (NB, NB),
}


def main_kernel(ids, ir_ref, ic_ref, a_ref, x_ref, li_ref, ui_ref, raw_ref, *refs):
    me = ids[0]
    count = len(KEPT)
    held_ref, here_ref, fetch_sem, store_sem = refs[2 * count :]
    far = dict(zip(KEPT, refs[:count]))
    near = dict(zip(KEPT, refs[count : 2 * count]))
    fetches = [
        pltpu.make_async_copy(raw_ref, held_ref, fetch_sem.at[0]),
        pltpu.make_async_copy(a_ref, here_ref, fetch_sem.at[1]),
    ]
    for fetch in fetches:
        fetch.start()
    stores = []

    def keep(name, value=None):
        if value is not None:
            near[name][...] = value
        stores.append(pltpu.make_async_copy(near[name], far[name], store_sem.at[len(stores)]))
        stores[-1].start()

    put = jnp.zeros((RD, 2 * NP), F32)
    lane = iota((NB, 2 * NP), 1)
    m = ((lane >> 1) & 7) * 4 + (lane >> 4)
    for g in range(2):
        own, loc = ir_ref[3 * g + 1 : 3 * g + 2, :], ir_ref[3 * g + 2 : 3 * g + 3, :]
        t = f((own == me) & (loc == iota((RD, NB), 0)))
        s = f(((ic_ref[:, 3 * g : 3 * g + 1] & 31) == m) & ((lane & 1) == g))
        put = put + bdot(t.astype(BF16), s.astype(BF16))
    keep("put", put)
    keep("back", jnp.concatenate([x_ref[x, 128:144, :] for x in range(4)], axis=0))
    slots = jnp.concatenate([x_ref[x, 0:128, :] for x in range(4)], axis=0)
    slot = iota((NB, 2 * NB), 1)
    new0 = pick2(f(ic_ref[:, 6:7] == slot), slots)
    keep("new0", new0[:, 0:NB])
    u0 = dot3(li_ref[0], new0)
    keep("u0", u0)
    new1 = pick2(f(ic_ref[:, 7:8] == slot), slots)
    keep("new1", new1[:, 0:NB])
    keep("lead1", dot3(li_ref[1], new1))
    fetches[0].wait()
    for n, name in enumerate(("low0", "end1")):
        raw = jnp.concatenate([held_ref[y, n] for y in range(8)], axis=0)
        keep(name, dot3(raw, ui_ref[n]))
    fetches[1].wait()
    for r in range(3):
        rows = pl.ds(NB * r, NB)
        near["base"][rows, :] = here_ref[rows, :] - dot3(near["low0"][rows, :], u0)
    keep("base")
    for store in stores:
        store.wait()


def own_kernel(ids, ic_ref, mine_ref, li_ref, ui_ref, out_ref):
    core = ids[3]
    slots = jnp.concatenate([mine_ref[x, 0:128] for x in range(4)], axis=0)
    for x in range(4):
        out_ref[NB + 16 * x : NB + 16 * x + 16, :] = mine_ref[x, 128:144]
    place = jnp.where(core == 0, ic_ref[:, 7:8], ic_ref[:, 6:7])
    new = pick2(f(place == iota((NB, 2 * NB), 1)), slots)

    @pl.when(core == 0)
    def _():
        out_ref[0:NB, :] = dot3(new, ui_ref[0])

    @pl.when(core == 1)
    def _():
        out_ref[0:NB, :] = dot3(dot3(li_ref[0], new), ui_ref[1])


def final_kernel(ids, own_ref, there_ref, li_ref, ui_ref, *refs):
    me, col, core = ids[0], ids[1], ids[3]
    count = len(KEPT)
    out_ref, done_ref, sem, fetch_sem = refs[count], *refs[2 * count + 1 :]
    near = dict(zip(KEPT, refs[count + 1 : 2 * count + 1]))
    fetches = {}
    order = ("u0", "lead1", "back", "low0", "end1", "put", "base", "new0", "new1")
    for n, name in enumerate(order):
        far = refs[list(KEPT).index(name)]
        fetches[name] = pltpu.make_async_copy(far, near[name], fetch_sem.at[n])
        fetches[name].start()
    own, there = own_ref[...], there_ref[...]
    sides = [jnp.where(core == k, own, there) for k in range(2)]
    diag, fill = sides[0][0:NB], sides[1][0:NB]
    rows_back = [v[NB : NB + 2 * NP] for v in sides]
    turn1 = dot3(li_ref[1], diag)
    low0_back = dot3(rows_back[0], ui_ref[0])
    low1_back = dot3(rows_back[1], ui_ref[1]) - dot3(low0_back, fill)
    for name in order[:3]:
        fetches[name].wait()
    u0 = near["u0"][...]
    u1 = near["lead1"][...] - dot3(turn1, u0)
    back = near["back"][...] - dot3(low0_back, u0) - dot3(low1_back, u1)
    for name in order[3:]:
        fetches[name].wait()
    copies = []
    for r in (2, 1, 0):
        rows = pl.ds(NB * r, NB)
        put = near["put"][rows, :]
        moved = sum_cols(put) > 0
        low0 = near["low0"][rows, :]
        low1 = near["end1"][rows, :] - dot3(low0, fill)
        done_ref[rows, :] = jnp.where(moved, pick2(put, back), near["base"][rows, :] - dot3(low1, u1))

        @pl.when(col == 0)
        def _():
            done_ref[rows, 0:NB] = jnp.where(moved, pick2(put, low0_back), low0)

        @pl.when(col == 1)
        def _():
            done_ref[rows, 0:NB] = jnp.where(moved, pick2(put, low1_back), low1)

        if r == 0:

            @pl.when(me == 0)
            def _():
                done_ref[0:NB, :] = u0

                @pl.when(col == 0)
                def _():
                    done_ref[0:NB, 0:NB] = near["new0"][...]

            @pl.when(me == 1)
            def _():
                done_ref[0:NB, :] = u1

                @pl.when(col == 0)
                def _():
                    done_ref[0:NB, 0:NB] = diag

                @pl.when(col == 1)
                def _():
                    done_ref[0:NB, 0:NB] = near["new1"][...] - dot3(diag, u0[:, 0:NB])

        copies.append(pltpu.make_async_copy(done_ref.at[rows, :], out_ref.at[rows, :], sem.at[r]))
        copies[-1].start()
    for copy in copies:
        copy.wait()


SCALAR = pl.BlockSpec(memory_space=pltpu.SMEM)


def call(kernel, outs, ids, *args, scratch=(), flops=0, far=(), far_out=False):
    vmem, anywhere = pl.BlockSpec(memory_space=pltpu.VMEM), pl.BlockSpec(memory_space=pl.ANY)
    smem = [] if ids is None else [SCALAR]
    sizes = [4 * o.size for o in jax.tree.leaves((outs, args))]
    return pl.pallas_call(
        kernel,
        out_shape=outs,
        in_specs=smem + [anywhere if n in far else vmem for n in range(len(args))],
        out_specs=jax.tree.map(lambda o: SCALAR if o.shape == (1,) else anywhere if far_out else vmem, outs),
        scratch_shapes=scratch,
        compiler_params=pltpu.CompilerParams(vmem_limit_bytes=(60 if far_out else 40) * 1024 * 1024),
        cost_estimate=pl.CostEstimate(flops=flops, bytes_accessed=min(sizes), transcendentals=0),
    )(*([] if ids is None else [ids]), *args)


def shape(*dims, dtype=F32):
    return jax.ShapeDtypeStruct(dims, dtype)


AROUND = (4, 3, 5, 2, 6, 1, 7)


def fast(matrix, pivots, lower_inv, upper_inv):
    prow_idx = lax.axis_index(PROW).astype(jnp.int32)
    pcol_idx = lax.axis_index(PCOL).astype(jnp.int32)
    y_idx, core_idx = lax.axis_index("y"), lax.axis_index("core")
    ids = jnp.stack([prow_idx, pcol_idx, y_idx, core_idx]).astype(jnp.int32)
    part = RD // 8
    rows, ir, ic, most, *panel = call(
        pack_kernel,
        (
            shape(NP, 5, 2, RD), shape(8, NB, dtype=jnp.int32), shape(NB, 8, dtype=jnp.int32),
            shape(1, dtype=jnp.int32), *[shape(part, NB)] * 8,
        ),
        ids, pivots, matrix, flops=10**6,
    )
    rows_in = lax.all_to_all(rows, PROW, 0, 0)
    piece = jnp.where(y_idx == 0, panel[0], F32(0.0))
    for k in AROUND:
        piece = piece + lax.ppermute(panel[k], "y", [(0, k)])
    rows_in, piece = lax.optimization_barrier((rows_in, piece))
    raw = lax.all_gather(piece, PCOL, tiled=True).reshape(8, 2, part, NB)
    send = call(
        turn_kernel, shape(8, 24, RD), ids, ir, ic, rows_in,
        scratch=[pltpu.VMEM((16, RD), F32), pltpu.VMEM((2 * NP, RD), F32)],
    )
    main_z = lax.all_to_all(send, "z", 0, 0)
    main_send, side = call(mid_kernel, (shape(4, 144, RD), shape(192, NB)), None, main_z)
    main_x = lax.all_to_all(main_send, "x", 0, 0)
    parts = [lax.ppermute(side, "y", [(0, k)]) for k in AROUND]
    side_send = call(
        side_kernel, shape(4, 144, NB), ids, side, *parts, scratch=[pltpu.VMEM((192, NB), F32)]
    )
    side_send, main_x, raw = lax.optimization_barrier((side_send, main_x, raw))
    mine = lax.all_to_all(side_send, "x", 0, 0)
    near = [pltpu.VMEM(dims, F32) for dims in KEPT.values()]
    kept = call(
        main_kernel, [shape(*dims) for dims in KEPT.values()],
        ids, ir, ic, matrix, main_x, lower_inv, upper_inv, raw, far=(2, 6), far_out=True,
        scratch=near + [
            pltpu.VMEM((8, 2, part, NB), F32), pltpu.VMEM((RD, RD), F32),
            pltpu.SemaphoreType.DMA((2,)), pltpu.SemaphoreType.DMA((len(KEPT),)),
        ],
    )
    mine, kept = lax.optimization_barrier((mine, kept))
    own = call(own_kernel, shape(NB + 2 * NP, NB), ids, ic, mine, lower_inv, upper_inv)
    there = lax.ppermute(own, "core", [(0, 1), (1, 0)])
    out = call(
        final_kernel, shape(RD, RD), ids, own, there, lower_inv, upper_inv, *kept,
        far=tuple(range(4, 4 + len(KEPT))), far_out=True,
        scratch=near + [
            pltpu.VMEM((RD, RD), F32), pltpu.SemaphoreType.DMA((3,)),
            pltpu.SemaphoreType.DMA((len(KEPT),)),
        ],
    )
    return out, most[0]


def broadcast(value, axis, root):
    mine = lax.axis_index(axis) == root
    return lax.psum(jnp.where(mine, value, jnp.zeros_like(value)), axis)


def general(matrix, pivots, lower_inv, upper_inv):
    current = matrix
    rows_dev = current.shape[0]
    cols_dev = current.shape[1]
    panel_width = pivots.shape[1]
    prow_idx = lax.axis_index(PROW)
    pcol_idx = lax.axis_index(PCOL)
    row_pos = jnp.arange(rows_dev)
    col_pos = jnp.arange(cols_dev)
    row_done = jnp.zeros((rows_dev,), bool)
    col_done = jnp.zeros((cols_dev,), bool)
    for panel_no in range(2):
        row_done = row_done | (prow_idx == panel_no) & (row_pos < panel_width)
        col_done = col_done | (pcol_idx == panel_no) & (col_pos < panel_width)
        pivot_list = pivots[panel_no]
        owner_row = pivot_list // rows_dev
        local_row = pivot_list % rows_dev
        is_owned = owner_row == prow_idx
        on_root = prow_idx == panel_no
        old_block = broadcast(current[:panel_width], PROW, panel_no)
        pivot_data = jnp.where(is_owned[:, None], current[local_row], F32(0.0))
        new_rows = lax.psum(pivot_data, PROW)
        upper_rows = hdot(lower_inv[panel_no], new_rows)
        row_block = jnp.where(col_done[None, :], new_rows, upper_rows)
        target = jnp.where(is_owned, local_row, rows_dev)
        current = current.at[target].set(old_block, mode="drop")
        current = current.at[:panel_width].set(jnp.where(on_root, row_block, current[:panel_width]))
        lower_here = hdot(current[:, :panel_width], upper_inv[panel_no])
        lower_cols = broadcast(lower_here, PCOL, panel_no)
        rank_update = hdot(lower_cols, row_block)
        keep_mask = (~row_done)[:, None] & (~col_done)[None, :]
        current = jnp.where(keep_mask, current - rank_update, current)
        panel_mask = (pcol_idx == panel_no) & (~row_done)[:, None]
        current = current.at[:, :panel_width].set(
            jnp.where(panel_mask, lower_cols, current[:, :panel_width])
        )
    return current


def local(matrix, pivots, lower_inv, upper_inv):
    def body(state):
        out = general(with_layout_constraint(matrix, ROW_MAJOR), pivots, lower_inv, upper_inv)
        return jnp.zeros((), bool), with_layout_constraint(out, ROW_MAJOR)

    quick, most = fast(matrix, pivots, lower_inv, upper_inv)
    return lax.while_loop(lambda state: state[0], body, (most > NP, quick))[1]


def solution(mesh):
    grid = Mesh(mesh.devices.reshape(8, 4, 8, 2), ("z", "x", "y", "core"))
    in_specs = (P(PROW, PCOL), P(), P(), P())
    return jax.shard_map(local, mesh=grid, in_specs=in_specs, out_specs=P(PROW, PCOL), check_vma=False)
```

```python
import functools

import jax
import jax.numpy as jnp
from jax import lax
from jax.experimental import pallas as pl
from jax.experimental.layout import Layout, with_layout_constraint
from jax.experimental.pallas import tpu as pltpu
from jax.sharding import Mesh, PartitionSpec as P

HIGHEST = lax.Precision.HIGHEST
F32 = jnp.float32
BF16 = jnp.bfloat16
NB = 256
RD = 768
PROW = ("z", "x")
PCOL = ("y", "core")
NP = 32
ROW_MAJOR = Layout((0, 1))


def hdot(a, b):
    return jnp.dot(a, b, precision=HIGHEST, preferred_element_type=F32)


def iota(shape, dim):
    return lax.broadcasted_iota(jnp.int32, shape, dim)


def f(mask):
    return jnp.where(mask, F32(1.0), F32(0.0))


def sum_rows(x):
    return jnp.sum(x, axis=0, keepdims=True)


def sum_cols(x):
    return jnp.sum(x, axis=1, keepdims=True)


def owner_of(row):
    return ((row >> 8) * 171) >> 9


def slot_of(rank, g):
    return ((rank & 3) * 128 + ((rank >> 2) & 7) * 16 + g * 8 + (rank >> 5)).astype(F32)


def index_math(pr, pc):
    p0r, p1r = pr[0:1, :], pr[1:2, :]
    p0c, p1c = pc
    sub, lane = iota((NB, NB), 0), iota((NB, NB), 1)
    lr, lc = iota((1, NB), 1), iota((NB, 1), 0)
    m_kj = f(p0c == lane + RD)
    n_kj = f(p0c == p1r)
    m_jk = f(p0r == sub + RD)
    n_jk = f(p0r == p1c)
    p1rf, p1cf = p1r.astype(F32), p1c.astype(F32)

    def dest(p0, p1, ids, has_m, has_n, piv_m, has_mk):
        stay0 = (p0 == ids) | (has_n > 0)
        end0 = jnp.where(has_m > 0, piv_m.astype(jnp.int32), p0)
        stay1 = (p1 == ids + RD) | (has_mk > 0)
        out = []
        for stay, end in ((stay0, end0), (stay1, p1)):
            own = owner_of(end)
            out.append((jnp.where(stay, NP, own), end - own * RD))
        return out

    has_m_c, has_n_c = sum_cols(m_kj), sum_cols(n_kj)
    has_m_r, has_n_r = sum_rows(m_jk), sum_rows(n_jk)
    has_mk_r, has_nk_r = sum_rows(m_kj), sum_rows(n_kj)
    has_mk_c, has_nk_c = sum_cols(m_jk), sum_cols(n_jk)
    dest_r = dest(p0r, p1r, lr, has_m_r, has_n_r, sum_rows(m_jk * p1cf), has_mk_r)
    dest_c = dest(p0c, p1c, lc, has_m_c, has_n_c, sum_cols(m_kj * p1rf), has_mk_c)
    ranks_r, ranks_c, pos_r, pos_c = [], [], [], []
    for g in range(2):
        key_r = dest_r[g][0] * NB + lr
        key_c = dest_c[g][0] * NB + lc
        rank_r = sum_rows(f(key_c < key_r)).astype(jnp.int32)
        rank_c = sum_cols(f(key_r < key_c)).astype(jnp.int32)
        ranks_r.append(rank_r)
        ranks_c.append(rank_c)
        pos_r.append(slot_of(rank_r, g))
        pos_c.append(slot_of(rank_c, g))
    w_r = jnp.where(has_mk_r > 0, sum_rows(m_kj * pos_c[0]), pos_r[1])
    w_c = jnp.where(has_mk_c > 0, sum_cols(m_jk * pos_r[0]), pos_c[1])
    src0 = jnp.where(
        has_m_c > 0,
        sum_cols(m_kj * pos_r[1]),
        jnp.where(has_n_c > 0, sum_cols(n_kj * w_r), pos_c[0]),
    )
    src1 = jnp.where(has_nk_c > 0, sum_cols(n_jk * pos_r[0]), w_c)
    rows, cols = [], []
    for g in range(2):
        rows += [ranks_r[g], dest_r[g][0], dest_r[g][1]]
        cols += [ranks_c[g], dest_c[g][0], dest_c[g][1]]
    cols += [src0.astype(jnp.int32), src1.astype(jnp.int32)]
    return rows, cols


def bdot(a, b):
    return jnp.dot(a, b, preferred_element_type=F32)


def halves(x):
    hi = x.astype(BF16)
    return hi, (x - hi.astype(F32)).astype(BF16)


def left3(a):
    hi, lo = halves(a)
    return jnp.concatenate([hi, hi, lo], axis=1)


def right3(b):
    hi, lo = halves(b)
    return jnp.concatenate([hi, lo, hi], axis=0)


def dot3(a, b):
    return bdot(left3(a), right3(b))


def pick2(p, x):
    p = p.astype(BF16)
    hi, lo = halves(x)
    return bdot(jnp.concatenate([p, p], axis=1), jnp.concatenate([hi, lo], axis=0))


def pick3(p, x):
    p = p.astype(BF16)
    hi = x.astype(BF16)
    rest = x - hi.astype(F32)
    mid = rest.astype(BF16)
    low = (rest - mid.astype(F32)).astype(BF16)
    return bdot(p, hi) + (bdot(p, mid) + bdot(p, low))


def pack_kernel(ids, p_ref, a_ref, send_ref, ir_ref, ic_ref, most_ref, *piece_refs):
    me = ids[0]
    for n, r in enumerate(piece_refs):
        rows_n = r.shape[0]
        r[...] = a_ref[rows_n * n : rows_n * (n + 1), 0:NB]
    pr = p_ref[...]
    eye = iota((NB, NB), 0) == iota((NB, NB), 1)
    turned = [sum_cols(jnp.where(eye, pr[n : n + 1, :].astype(F32), F32(0.0))) for n in range(2)]
    rows, cols = index_math(pr, [t.astype(jnp.int32) for t in turned])
    for n, v in enumerate(rows):
        ir_ref[n : n + 1, :] = v
    ir_ref[6:8, :] = jnp.zeros((2, NB), jnp.int32)
    for n, v in enumerate(cols):
        ic_ref[:, n : n + 1] = v
    counts = [sum_rows(f(cols[3 * g + 1] == iota((NB, NP), 1))) for g in range(2)]
    most_ref[0] = jnp.max(jnp.maximum(counts[0], counts[1])).astype(jnp.int32)
    line = iota((NB, NB), 0)
    rank = jnp.where(me == 1, rows[3], rows[0])
    perm = f(rank == (line >> 3) + NP * (line & 7))
    old = pick3(perm, a_ref[0:NB, :])
    line = iota((2 * NP, NB), 0)
    pick = jnp.zeros((2 * NP, RD), F32)
    for g in range(2):
        rank, own = rows[3 * g], rows[3 * g + 1]
        s = f(((line & 1) == g) & ((rank & 31) == (line >> 1)) & (own == me))
        t = f(cols[3 * g + 2] == iota((NB, RD), 1))
        pick = pick + bdot(s.astype(BF16), t.astype(BF16))
    ext = pick3(pick, a_ref[...])
    for m in range(NP):
        for q in range(4):
            send_ref[m, q] = old[8 * m + 2 * q : 8 * m + 2 * q + 2]
        send_ref[m, 4] = ext[2 * m : 2 * m + 2]


def turn_kernel(ids, ir_ref, ic_ref, in_ref, send_ref, old_ref, ext_ref):
    me = ids[0]
    for q in range(4):
        old_ref[2 * q : 2 * q + 2, :] = in_ref[0, q]
        old_ref[8 + 2 * q : 10 + 2 * q, :] = in_ref[1, q]
    for m in range(NP):
        ext_ref[2 * m : 2 * m + 2, :] = in_ref[m, 4]
    line = iota((16, NB), 0)
    want = me + NP * (line & 7)
    own = jnp.zeros((16, 1), F32)
    for g in range(2):
        hit = f((ir_ref[3 * g : 3 * g + 1, :] == want) & ((line >> 3) == g))
        own = own + sum_cols(hit * ir_ref[3 * g + 1 : 3 * g + 2, :].astype(F32))
    own = own.astype(jnp.int32)
    old = old_ref[...]
    lane = iota((16, 2 * NP), 1)
    pick = f((own == (lane >> 1)) & ((iota((16, 2 * NP), 0) >> 3) == (lane & 1)))
    slots = jnp.where(own == NP, old, pick3(pick, ext_ref[...]))
    want = me + NP * (iota((NB, 16), 1) & 7)
    own = jnp.zeros((1, 16), F32)
    for g in range(2):
        hit = f((ic_ref[:, 3 * g : 3 * g + 1] == want) & ((iota((NB, 16), 1) >> 3) == g))
        own = own + sum_rows(hit * ic_ref[:, 3 * g + 1 : 3 * g + 2].astype(F32))
    own = own.astype(jnp.int32)
    line = iota((2 * NP, 16), 0)
    give = f((own == (line >> 1)) & ((iota((2 * NP, 16), 1) >> 3) == (line & 1)))
    back = pick3(give, old)
    for z in range(8):
        send_ref[z, 0:16, :] = slots
        send_ref[z, 16:24, :] = back[8 * z : 8 * z + 8]


def arrange(get, out_ref):
    for x in range(4):
        for z in range(8):
            out_ref[x, 16 * z : 16 * z + 16, :] = get(z, 0, 16)
            out_ref[x, 128 + 2 * z : 130 + 2 * z, :] = get(z, 16 + 2 * x, 18 + 2 * x)


def mid_kernel(in_ref, out_ref, side_ref):
    arrange(lambda z, a, b: in_ref[z, a:b, :], out_ref)
    for z in range(8):
        side_ref[24 * z : 24 * z + 24, :] = in_ref[z, :, 0:NB]


def side_kernel(ids, *refs):
    own, out, sums = refs[0], refs[8], refs[9]
    total = jnp.where(ids[2] == 0, own[...], F32(0.0))
    for r in refs[1:8]:
        total = total + r[...]
    sums[...] = total
    arrange(lambda z, a, b: sums[24 * z + a : 24 * z + b, :], out)


KEPT = {
    "base": (RD, RD), "lead1": (NB, RD), "u0": (NB, RD), "low0": (RD, NB), "end1": (RD, NB),
    "put": (RD, 4 * NP), "back": (2 * NP, RD), "new0": (NB, NB), "new1": (NB, NB),
}


def main_kernel(ids, ir_ref, ic_ref, a_ref, x_ref, li_ref, ui_ref, raw_ref, *refs):
    me = ids[0]
    count = len(KEPT)
    held_ref, here_ref, fetch_sem, store_sem = refs[2 * count :]
    far = dict(zip(KEPT, refs[:count]))
    near = dict(zip(KEPT, refs[count : 2 * count]))
    fetches = [
        pltpu.make_async_copy(raw_ref, held_ref, fetch_sem.at[0]),
        pltpu.make_async_copy(a_ref, here_ref, fetch_sem.at[1]),
    ]
    for fetch in fetches:
        fetch.start()
    stores = []

    def keep(name, value=None):
        if value is not None:
            near[name][...] = value
        stores.append(pltpu.make_async_copy(near[name], far[name], store_sem.at[len(stores)]))
        stores[-1].start()

    put = jnp.zeros((RD, 4 * NP), F32)
    lane = iota((NB, 4 * NP), 1) & 63
    m = ((lane >> 1) & 7) * 4 + (lane >> 4)
    for g in range(2):
        own, loc = ir_ref[3 * g + 1 : 3 * g + 2, :], ir_ref[3 * g + 2 : 3 * g + 3, :]
        t = f((own == me) & (loc == iota((RD, NB), 0)))
        s = f(((ic_ref[:, 3 * g : 3 * g + 1] & 31) == m) & ((lane & 1) == g))
        put = put + bdot(t.astype(BF16), s.astype(BF16))
    keep("put", put)
    keep("back", jnp.concatenate([x_ref[x, 128:144, :] for x in range(4)], axis=0))
    slots = jnp.concatenate([x_ref[x, 0:128, :] for x in range(4)], axis=0)
    slot = iota((NB, 2 * NB), 1)
    new0 = pick2(f(ic_ref[:, 6:7] == slot), slots)
    keep("new0", new0[:, 0:NB])
    u0 = dot3(li_ref[0], new0)
    keep("u0", u0)
    new1 = pick2(f(ic_ref[:, 7:8] == slot), slots)
    keep("new1", new1[:, 0:NB])
    keep("lead1", dot3(li_ref[1], new1))
    fetches[0].wait()
    for n, name in enumerate(("low0", "end1")):
        raw = jnp.concatenate([held_ref[y, n] for y in range(8)], axis=0)
        keep(name, dot3(raw, ui_ref[n]))
    fetches[1].wait()
    by_u0 = right3(u0)
    for r in range(3):
        rows = pl.ds(NB * r, NB)
        near["base"][rows, :] = here_ref[rows, :] - bdot(left3(near["low0"][rows, :]), by_u0)
    keep("base")
    for store in stores:
        store.wait()


def final_kernel(ids, ic_ref, mine_ref, there_ref, li_ref, ui_ref, *refs):
    me, col, core = ids[0], ids[1], ids[3]
    count = len(KEPT)
    out_ref, done_ref, sem, fetch_sem = refs[count], *refs[2 * count + 1 :]
    near = dict(zip(KEPT, refs[count + 1 : 2 * count + 1]))
    fetches = {}
    order = ("u0", "lead1", "back", "low0", "end1", "put", "base", "new0", "new1")
    for n, name in enumerate(order):
        far = refs[list(KEPT).index(name)]
        fetches[name] = pltpu.make_async_copy(far, near[name], fetch_sem.at[n])
        fetches[name].start()
    mine, there = mine_ref[...], there_ref[...]
    sides = [jnp.where(core == k, mine, there) for k in range(2)]
    slots = [jnp.concatenate([v[x, 0:128] for x in range(4)], axis=0) for v in sides]
    rows_back = [jnp.concatenate([v[x, 128:144] for x in range(4)], axis=0) for v in sides]
    slot = iota((NB, 2 * NB), 1)
    diag = dot3(pick2(f(ic_ref[:, 7:8] == slot), slots[0]), ui_ref[0])
    new0_c1 = pick2(f(ic_ref[:, 6:7] == slot), slots[1])
    fill = dot3(dot3(li_ref[0], new0_c1), ui_ref[1])
    low0_back = dot3(rows_back[0], ui_ref[0])
    low1_back = dot3(rows_back[1], ui_ref[1]) - dot3(low0_back, fill)
    for name in order[:3]:
        fetches[name].wait()
    u0 = near["u0"][...]
    by_u0 = right3(u0)
    u1 = near["lead1"][...] - bdot(left3(dot3(li_ref[1], diag)), by_u0)
    by_u1 = right3(u1)
    back = near["back"][...] - bdot(left3(low0_back), by_u0) - bdot(left3(low1_back), by_u1)
    by_u1 = jnp.concatenate([by_u1, *halves(-back)], axis=0)
    by_fill = jnp.concatenate([right3(fill), *halves(-low1_back)], axis=0)
    by_low0 = jnp.concatenate(halves(low0_back), axis=0)
    for name in order[3:]:
        fetches[name].wait()
    copies = []
    for r in (2, 1, 0):
        rows = pl.ds(NB * r, NB)
        put = near["put"][rows, :]
        moved = sum_cols(put) > 0
        put = put.astype(BF16)
        low0 = near["low0"][rows, :]
        stay0 = jnp.where(moved, F32(0.0), low0)
        low1 = jnp.where(moved, F32(0.0), near["end1"][rows, :]) - bdot(
            jnp.concatenate([left3(stay0), put], axis=1), by_fill
        )
        stay1 = jnp.where(moved, F32(0.0), low1)
        done_ref[rows, :] = jnp.where(moved, F32(0.0), near["base"][rows, :]) - bdot(
            jnp.concatenate([left3(stay1), put], axis=1), by_u1
        )

        @pl.when(col == 0)
        def _():
            done_ref[rows, 0:NB] = stay0 + bdot(put, by_low0)

        @pl.when(col == 1)
        def _():
            done_ref[rows, 0:NB] = low1

        if r == 0:

            @pl.when(me == 0)
            def _():
                done_ref[0:NB, :] = u0

                @pl.when(col == 0)
                def _():
                    done_ref[0:NB, 0:NB] = near["new0"][...]

            @pl.when(me == 1)
            def _():
                done_ref[0:NB, :] = u1

                @pl.when(col == 0)
                def _():
                    done_ref[0:NB, 0:NB] = diag

                @pl.when(col == 1)
                def _():
                    done_ref[0:NB, 0:NB] = near["new1"][...] - dot3(diag, u0[:, 0:NB])

        copies.append(pltpu.make_async_copy(done_ref.at[rows, :], out_ref.at[rows, :], sem.at[r]))
        copies[-1].start()
    for copy in copies:
        copy.wait()


SCALAR = pl.BlockSpec(memory_space=pltpu.SMEM)


def call(kernel, outs, ids, *args, scratch=(), flops=0, far=(), far_out=False):
    vmem, anywhere = pl.BlockSpec(memory_space=pltpu.VMEM), pl.BlockSpec(memory_space=pl.ANY)
    smem = [] if ids is None else [SCALAR]
    sizes = [4 * o.size for o in jax.tree.leaves((outs, args))]
    return pl.pallas_call(
        kernel,
        out_shape=outs,
        in_specs=smem + [anywhere if n in far else vmem for n in range(len(args))],
        out_specs=jax.tree.map(lambda o: SCALAR if o.shape == (1,) else anywhere if far_out else vmem, outs),
        scratch_shapes=scratch,
        compiler_params=pltpu.CompilerParams(vmem_limit_bytes=(60 if far_out else 40) * 1024 * 1024),
        cost_estimate=pl.CostEstimate(flops=flops, bytes_accessed=min(sizes), transcendentals=0),
    )(*([] if ids is None else [ids]), *args)


def shape(*dims, dtype=F32):
    return jax.ShapeDtypeStruct(dims, dtype)


AROUND = (4, 3, 5, 2, 6, 1, 7)


def fast(matrix, pivots, lower_inv, upper_inv):
    prow_idx = lax.axis_index(PROW).astype(jnp.int32)
    pcol_idx = lax.axis_index(PCOL).astype(jnp.int32)
    y_idx, core_idx = lax.axis_index("y"), lax.axis_index("core")
    ids = jnp.stack([prow_idx, pcol_idx, y_idx, core_idx]).astype(jnp.int32)
    part = RD // 8
    rows, ir, ic, most, *panel = call(
        pack_kernel,
        (
            shape(NP, 5, 2, RD), shape(8, NB, dtype=jnp.int32), shape(NB, 8, dtype=jnp.int32),
            shape(1, dtype=jnp.int32), *[shape(part, NB)] * 8,
        ),
        ids, pivots, matrix, flops=10**6,
    )
    rows_in = lax.all_to_all(rows, PROW, 0, 0)
    piece = jnp.where(y_idx == 0, panel[0], F32(0.0))
    for k in AROUND:
        piece = piece + lax.ppermute(panel[k], "y", [(0, k)])
    rows_in, piece = lax.optimization_barrier((rows_in, piece))
    raw = lax.all_gather(piece, PCOL, tiled=True).reshape(8, 2, part, NB)
    send = call(
        turn_kernel, shape(8, 24, RD), ids, ir, ic, rows_in,
        scratch=[pltpu.VMEM((16, RD), F32), pltpu.VMEM((2 * NP, RD), F32)],
    )
    main_z = lax.all_to_all(send, "z", 0, 0)
    main_send, side = call(mid_kernel, (shape(4, 144, RD), shape(192, NB)), None, main_z)
    main_x = lax.all_to_all(main_send, "x", 0, 0)
    parts = [lax.ppermute(side, "y", [(0, k)]) for k in AROUND]
    side_send = call(
        side_kernel, shape(4, 144, NB), ids, side, *parts, scratch=[pltpu.VMEM((192, NB), F32)]
    )
    side_send, main_x, raw = lax.optimization_barrier((side_send, main_x, raw))
    mine = lax.all_to_all(side_send, "x", 0, 0)
    near = [pltpu.VMEM(dims, F32) for dims in KEPT.values()]
    kept = call(
        main_kernel, [shape(*dims) for dims in KEPT.values()],
        ids, ir, ic, matrix, main_x, lower_inv, upper_inv, raw, far=(2, 6), far_out=True,
        scratch=near + [
            pltpu.VMEM((8, 2, part, NB), F32), pltpu.VMEM((RD, RD), F32),
            pltpu.SemaphoreType.DMA((2,)), pltpu.SemaphoreType.DMA((len(KEPT),)),
        ],
    )
    mine, kept = lax.optimization_barrier((mine, kept))
    there = lax.ppermute(mine, "core", [(0, 1), (1, 0)])
    out = call(
        final_kernel, shape(RD, RD), ids, ic, mine, there, lower_inv, upper_inv, *kept,
        far=tuple(range(5, 5 + len(KEPT))), far_out=True,
        scratch=near + [
            pltpu.VMEM((RD, RD), F32), pltpu.SemaphoreType.DMA((3,)),
            pltpu.SemaphoreType.DMA((len(KEPT),)),
        ],
    )
    return out, most[0]


def broadcast(value, axis, root):
    mine = lax.axis_index(axis) == root
    return lax.psum(jnp.where(mine, value, jnp.zeros_like(value)), axis)


def general(matrix, pivots, lower_inv, upper_inv):
    current = matrix
    rows_dev = current.shape[0]
    cols_dev = current.shape[1]
    panel_width = pivots.shape[1]
    prow_idx = lax.axis_index(PROW)
    pcol_idx = lax.axis_index(PCOL)
    row_pos = jnp.arange(rows_dev)
    col_pos = jnp.arange(cols_dev)
    row_done = jnp.zeros((rows_dev,), bool)
    col_done = jnp.zeros((cols_dev,), bool)
    for panel_no in range(2):
        row_done = row_done | (prow_idx == panel_no) & (row_pos < panel_width)
        col_done = col_done | (pcol_idx == panel_no) & (col_pos < panel_width)
        pivot_list = pivots[panel_no]
        owner_row = pivot_list // rows_dev
        local_row = pivot_list % rows_dev
        is_owned = owner_row == prow_idx
        on_root = prow_idx == panel_no
        old_block = broadcast(current[:panel_width], PROW, panel_no)
        pivot_data = jnp.where(is_owned[:, None], current[local_row], F32(0.0))
        new_rows = lax.psum(pivot_data, PROW)
        upper_rows = hdot(lower_inv[panel_no], new_rows)
        row_block = jnp.where(col_done[None, :], new_rows, upper_rows)
        target = jnp.where(is_owned, local_row, rows_dev)
        current = current.at[target].set(old_block, mode="drop")
        current = current.at[:panel_width].set(jnp.where(on_root, row_block, current[:panel_width]))
        lower_here = hdot(current[:, :panel_width], upper_inv[panel_no])
        lower_cols = broadcast(lower_here, PCOL, panel_no)
        rank_update = hdot(lower_cols, row_block)
        keep_mask = (~row_done)[:, None] & (~col_done)[None, :]
        current = jnp.where(keep_mask, current - rank_update, current)
        panel_mask = (pcol_idx == panel_no) & (~row_done)[:, None]
        current = current.at[:, :panel_width].set(
            jnp.where(panel_mask, lower_cols, current[:, :panel_width])
        )
    return current


def local(matrix, pivots, lower_inv, upper_inv):
    def body(state):
        out = general(with_layout_constraint(matrix, ROW_MAJOR), pivots, lower_inv, upper_inv)
        return jnp.zeros((), bool), with_layout_constraint(out, ROW_MAJOR)

    quick, most = fast(matrix, pivots, lower_inv, upper_inv)
    return lax.while_loop(lambda state: state[0], body, (most > NP, quick))[1]


def solution(mesh):
    grid = Mesh(mesh.devices.reshape(8, 4, 8, 2), ("z", "x", "y", "core"))
    in_specs = (P(PROW, PCOL), P(), P(), P())
    return jax.shard_map(local, mesh=grid, in_specs=in_specs, out_specs=P(PROW, PCOL), check_vma=False)
```
